512 devices in a mesh: lat: 8 (over y, z_hi), lon: 64 (over x, z_lo, core).
Axes of the slice: x: 4, y: 4, z: 16 (z_hi: 2, z_lo: 8; z = z_hi * 8 + z_lo), core: 2. Of those that a mesh axis runs over, the one named last changes fastest.
Arguments:
- activations: bfloat16 [2, 48, 768, 192], P(None, 'lat', 'lon'), may hold values from -400 to 400
- cotangent: bfloat16 [2, 48, 768, 192], P(None, 'lat', 'lon'), may hold values from -12 to 12
- gain: float32 [192], replicated, may hold values from 0.5 to 1.5
- w_qkv: bfloat16 [192, 576], replicated, may hold values from -0.4375 to 0.4375
- w_proj: bfloat16 [192, 192], replicated, may hold values from -0.4375 to 0.4375
- bias_table: float32 [8, 6, 3312], P('lat'), may hold values from -3 to 325
- regions: int32 [2, 48, 768], P(None, 'lat', 'lon'), may hold values from 0 to 3
Outputs:
- grad_input: bfloat16 [2, 48, 768, 192], P(None, 'lat', 'lon')
- grad_qkv: float32 [192, 576], replicated
- grad_proj: float32 [192, 192], replicated
- grad_gain: float32 [192], replicated
- grad_table: float32 [8, 6, 3312], P('lat')
The draws below stay inside these ranges and needn't reach their ends.
All inputs are finite; a program needn't handle non-finite values.
Results may differ from the reference program's by a relative error of at most 0.0094.
The reference program's roundings to bfloat16 on the way count: a program that leaves them out, or rounds other values in their place, can miss the bound.
Values may be sent and summed in bfloat16 or wider, within the bound.
A program may use at most 64 MiB of HBM per device.

```python
import math
import jax
import jax.numpy as jnp
from jax import lax

WIDTH = 192
HEADS = 6
LEVELS = 2
WIN_LAT = 6
WIN_LON = 12
WIN_TOK = 144
SHIFT_LAT = 3
SHIFT_LON = 6
REL = 3312
NLAT = 48
NLON = 768
BANDS = 8
LONWIN = 64


def draw_activations(key, part):
    key = jax.random.fold_in(key, 11)
    subkeys = jax.random.split(key, 3)
    chan_scale = jnp.exp(jax.random.uniform(subkeys[0], (WIDTH,), jnp.float32, 0.0, math.log(10.0)))
    token_scale = jnp.exp(jax.random.uniform(subkeys[1], (LEVELS, NLAT, NLON, 1), jnp.float32, 0.0, math.log(10.0)))
    sample = jnp.clip(jax.random.normal(subkeys[2], (LEVELS, NLAT, NLON, WIDTH), jnp.float32), -4.0, 4.0)
    return (sample * chan_scale * token_scale).astype(jnp.bfloat16)


def draw_cotangent(key, part):
    key = jax.random.fold_in(key, 12)
    subkeys = jax.random.split(key, 1)
    lat_weight = 1.0 + 2.0 * jnp.arange(NLAT, dtype=jnp.float32) / (NLAT - 1)
    lat_weight = lat_weight[None, :, None, None]
    sample = jnp.clip(jax.random.normal(subkeys[0], (LEVELS, NLAT, NLON, WIDTH), jnp.float32), -4.0, 4.0)
    return (sample * lat_weight).astype(jnp.bfloat16)


def draw_bias_table(key, part):
    key = jax.random.fold_in(key, 13)
    subkeys = jax.random.split(key, 1)
    sample = jnp.clip(jax.random.normal(subkeys[0], (BANDS, HEADS, REL), jnp.float32), -3.0, 3.0)
    return sample.astype(jnp.float32)


def with_ends(array, own_key, smallest, top_value):
    index_at = [jax.random.randint(jax.random.fold_in(own_key, axis), (), 0, length) for axis, length in enumerate(array.shape)]
    widest = array.shape.index(max(array.shape))
    neighbour = index_at[:widest] + [(index_at[widest] + 1) % array.shape[widest]] + index_at[widest + 1:]
    return array.at[tuple(index_at)].set(smallest).at[tuple(neighbour)].set(top_value)


def normal_values(rng, shape, spread, limit, kind=jnp.bfloat16):
    values = jax.random.normal(rng, shape, jnp.float32) * spread
    return jnp.minimum(jnp.maximum(values, -limit), limit).astype(kind)


def setup_inputs(seed: int = 0) -> dict:
    keys = jax.random.split(jax.random.key(seed), 8)
    return {
        "activations": draw_activations(jax.random.fold_in(keys[7], 71), 0),
        "cotangent": draw_cotangent(jax.random.fold_in(keys[7], 71), 0),
        "gain": jnp.clip(1.0 + 0.1 * jax.random.normal(keys[2], (WIDTH,), jnp.float32), 0.5, 1.5),
        "w_qkv": normal_values(keys[3], (WIDTH, 3 * WIDTH), WIDTH ** -0.5, 0.4375),
        "w_proj": normal_values(keys[4], (WIDTH, WIDTH), WIDTH ** -0.5, 0.4375),
        "bias_table": draw_bias_table(jax.random.fold_in(keys[7], 71), 0),
        "regions": with_ends(jax.random.randint(keys[6], (LEVELS, NLAT, NLON), 0, 4), jax.random.fold_in(keys[6], 1), 0, 3).astype(jnp.int32),
    }


eps_norm = 1e-05
eps_rms = 1e-06

def pair_index():
    token_ids = jnp.arange(LEVELS * WIN_LAT * WIN_LON, dtype=jnp.int32)
    level_ids = token_ids // (WIN_LAT * WIN_LON)
    row_ids = token_ids // WIN_LON % WIN_LAT
    col_ids = token_ids % WIN_LON
    first_part = (level_ids[:, None] * LEVELS + level_ids[None, :]) * (WIN_LAT * WIN_LAT) + row_ids[:, None] * WIN_LAT + row_ids[None, :]
    return (first_part * (2 * WIN_LON - 1) + col_ids[None, :] - col_ids[:, None] + WIN_LON - 1).reshape(-1)

def to_windows(field_data):
    level_count, row_count, col_count = (field_data.shape[0], field_data.shape[1], field_data.shape[2])
    tail_dims = field_data.shape[3:]
    field_data = field_data.reshape((level_count, row_count // WIN_LAT, WIN_LAT, col_count // WIN_LON, WIN_LON) + tail_dims)
    axis_order = (1, 3, 0, 2, 4) + tuple(range(5, 5 + len(tail_dims)))
    field_data = field_data.transpose(axis_order)
    return field_data.reshape((row_count // WIN_LAT * (col_count // WIN_LON), level_count * WIN_LAT * WIN_LON) + tail_dims)

def from_windows(windows, row_count, col_count):
    level_count = windows.shape[1] // (WIN_LAT * WIN_LON)
    tail_dims = windows.shape[2:]
    field_data = windows.reshape((row_count // WIN_LAT, col_count // WIN_LON, level_count, WIN_LAT, WIN_LON) + tail_dims)
    axis_order = (2, 0, 3, 1, 4) + tuple(range(5, 5 + len(tail_dims)))
    return field_data.transpose(axis_order).reshape((level_count, row_count, col_count) + tail_dims)

def window_grads(wins_x, wins_g, wins_region, wins_bias, gain, w_qkv, w_proj):
    win_count, token_count, feat_width = wins_x.shape
    head_count = wins_bias.shape[1]
    head_dim = feat_width // head_count
    pair_ids = pair_index()
    inputs = wins_x.astype(jnp.float32)
    row_mean = lax.optimization_barrier(jnp.mean(inputs, axis=-1, keepdims=True))
    centred = inputs - row_mean
    inv_std = lax.rsqrt(lax.optimization_barrier(jnp.mean(centred * centred, axis=-1, keepdims=True)) + eps_norm)
    standard = centred * inv_std
    normed = (standard * gain).astype(jnp.bfloat16)
    flat_normed = normed.reshape(-1, feat_width)
    projected = lax.optimization_barrier(jnp.dot(flat_normed, w_qkv, preferred_element_type=jnp.float32).astype(jnp.bfloat16))
    projected = projected.reshape(win_count, token_count, 3, head_count, head_dim)
    queries = projected[:, :, 0].astype(jnp.float32)
    key_vecs = projected[:, :, 1].astype(jnp.float32)
    val_vecs = projected[:, :, 2].astype(jnp.float32)
    score_scale = head_dim ** (-0.5)
    scores = jnp.einsum('nihd,njhd->nhij', queries, key_vecs) * score_scale
    scores = scores + wins_bias[:, :, pair_ids].reshape(win_count, head_count, token_count, token_count)
    same_region = wins_region[:, None, :, None] == wins_region[:, None, None, :]
    scores = jnp.where(same_region, scores, -1e+30)
    row_max = lax.optimization_barrier(jnp.max(scores, axis=-1, keepdims=True))
    exp_scores = jnp.exp(scores - row_max)
    attn_probs = exp_scores / lax.optimization_barrier(jnp.sum(exp_scores, axis=-1, keepdims=True))
    probs_low = lax.optimization_barrier(attn_probs.astype(jnp.bfloat16)).astype(jnp.float32)
    mixed = jnp.einsum('nhij,njhd->nihd', probs_low, val_vecs).astype(jnp.bfloat16).reshape(-1, feat_width)
    grad_out = wins_g.reshape(-1, feat_width)
    grad_proj = jnp.dot(mixed.T, grad_out, preferred_element_type=jnp.float32)
    grad_mixed = lax.optimization_barrier(jnp.dot(grad_out, w_proj.T, preferred_element_type=jnp.float32).astype(jnp.bfloat16))
    grad_mixed = grad_mixed.astype(jnp.float32).reshape(win_count, token_count, head_count, head_dim)
    grad_probs = jnp.einsum('nihd,njhd->nhij', grad_mixed, val_vecs)
    grad_values = jnp.einsum('nhij,nihd->njhd', probs_low, grad_mixed).astype(jnp.bfloat16)
    grad_scores = attn_probs * (grad_probs - lax.optimization_barrier(jnp.sum(attn_probs * grad_probs, axis=-1, keepdims=True)))
    grad_queries = (jnp.einsum('nhij,njhd->nihd', grad_scores, key_vecs) * score_scale).astype(jnp.bfloat16)
    grad_keys = (jnp.einsum('nhij,nihd->njhd', grad_scores, queries) * score_scale).astype(jnp.bfloat16)
    grad_proj_in = jnp.stack([grad_queries, grad_keys, grad_values], axis=2).reshape(-1, 3 * feat_width)
    grad_qkv = jnp.dot(flat_normed.T, grad_proj_in, preferred_element_type=jnp.float32)
    grad_normed = jnp.dot(grad_proj_in, w_qkv.T, preferred_element_type=jnp.float32).reshape(win_count, token_count, feat_width)
    grad_gain = lax.optimization_barrier(jnp.sum(grad_normed * standard, axis=(0, 1)))
    grad_std = grad_normed * gain
    grad_x = inv_std * (grad_std - lax.optimization_barrier(jnp.mean(grad_std, axis=-1, keepdims=True)) - standard * lax.optimization_barrier(jnp.mean(grad_std * standard, axis=-1, keepdims=True)))
    return (grad_x.astype(jnp.bfloat16), grad_qkv, grad_proj, grad_gain, grad_scores.reshape(win_count, head_count, -1))

def rescale(grad_value):
    return grad_value / jnp.sqrt(jnp.mean(grad_value * grad_value) + eps_rms)

def reference(activations, cotangent, gain, w_qkv, w_proj, bias_table, regions):
    rolled = jnp.roll(activations, (-1, -SHIFT_LAT, -SHIFT_LON), axis=(0, 1, 2))
    rolled_grad = jnp.roll(cotangent, (-1, -SHIFT_LAT, -SHIFT_LON), axis=(0, 1, 2))
    pair_count = WIN_TOK * WIN_TOK

    def one_row(totals, row_index):
        row_start = row_index * WIN_LAT
        slab_x = to_windows(lax.dynamic_slice_in_dim(rolled, row_start, WIN_LAT, 1))
        slab_g = to_windows(lax.dynamic_slice_in_dim(rolled_grad, row_start, WIN_LAT, 1))
        slab_r = to_windows(lax.dynamic_slice_in_dim(regions, row_start, WIN_LAT, 1))
        row_bias = lax.dynamic_index_in_dim(bias_table, row_index, 0, keepdims=False)
        slab_bias = jnp.broadcast_to(row_bias[None], (LONWIN,) + row_bias.shape)
        grad_x, grad_qkv, grad_proj, grad_gain, grad_pairs = window_grads(slab_x, slab_g, slab_r, slab_bias, gain, w_qkv, w_proj)
        band_sums = totals[3].at[row_index].add(lax.optimization_barrier(jnp.sum(grad_pairs, axis=0)))
        return ((totals[0] + grad_qkv, totals[1] + grad_proj, totals[2] + grad_gain, band_sums), from_windows(grad_x, WIN_LAT, NLON))
    start_totals = (jnp.zeros((WIDTH, 3 * WIDTH), jnp.float32), jnp.zeros((WIDTH, WIDTH), jnp.float32), jnp.zeros((WIDTH,), jnp.float32), jnp.zeros((BANDS, HEADS, pair_count), jnp.float32))
    totals, slabs = lax.scan(one_row, start_totals, jnp.arange(BANDS, dtype=jnp.int32))
    grad_rolled = slabs.transpose(1, 0, 2, 3, 4).reshape(LEVELS, NLAT, NLON, WIDTH)
    unrolled = jnp.roll(grad_rolled, (1, SHIFT_LAT, SHIFT_LON), axis=(0, 1, 2))
    grad_input = (cotangent.astype(jnp.float32) + unrolled.astype(jnp.float32)).astype(jnp.bfloat16)
    table_raw = jnp.zeros((BANDS, HEADS, REL), jnp.float32).at[:, :, pair_index()].add(totals[3])
    return (grad_input, rescale(totals[0]), rescale(totals[1]), rescale(totals[2]), rescale(table_raw))
```

```python
import functools

import jax
import jax.numpy as jnp
import ml_dtypes
import numpy as np
from jax import lax
from jax.experimental import pallas as pl
from jax.experimental.pallas import tpu as pltpu
from jax.sharding import PartitionSpec as P

F32 = jnp.float32
BF = jnp.bfloat16
MESH = pl.DeviceIdType.MESH

EPS_NORM = 1e-05
EPS_RMS = 1e-06
SCALE = 32.0 ** -0.5

NX, NY, ZHI, ZLO = 4, 4, 2, 8
NZ = ZHI * ZLO
NXY = NX * NY
NLAT = NY * ZHI
NCX = NX * 2


def tables():
    pack = np.zeros((3, 448, 192), np.float32)
    unpack = np.zeros((3, 144, 448), np.float32)
    ret = np.zeros((3, 256, 144), np.float32)
    home = np.zeros((3, 192, 256), np.float32)
    for ah in range(2):
        for bh in range(2):
            q = ah * 2 + bh
            for l in range(2):
                for a3 in range(3):
                    for b6 in range(6):
                        k = l * 18 + a3 * 6 + b6
                        i = a3 + (0 if ah else 3)
                        j = b6 + (0 if bh else 6)
                        src = ((1 - l) * 6 + i) * 16 + j
                        tok = (bh * 6 + b6) * 12 + l * 6 + ah * 3 + a3
                        for c in range(3):
                            pack[c, q * 112 + c * 36 + k, src] = 1
                            unpack[c, tok, q * 112 + c * 36 + k] = 1
                        ret[0, q * 64 + k, tok] = 1
                        home[0, src, q * 64 + k] = 1
                        part = 1 if k < 18 else 2
                        row = q * 64 + 36 + k % 18
                        ret[part, row, tok] = 1
                        home[part, src, row] = 1
    rep = np.zeros((864, 144), np.float32)
    rep[np.arange(864), np.arange(864) // 6] = 1
    heads = np.zeros((864, 192), np.float32)
    heads[np.arange(864)[:, None] % 6 == np.arange(192)[None, :] // 32] = 1
    shift = np.zeros((12, 144, 384), np.float32)
    for bs in range(12):
        for bt in range(12):
            for la in range(12):
                shift[bs, bt * 12 + la, la * 23 + bt - bs + 11] = 1
    rows = np.zeros((192, 256), np.float32)
    for c in range(192):
        rows[c, c // 12 * 16 + c % 12] = 1
    trows = np.zeros((128, 72), np.float32)
    for r in range(72):
        trows[r // 9 * 16 + r % 9, r] = 1
    col = np.zeros((12, 144), np.float32)
    col[np.arange(144) // 12, np.arange(144)] = 1
    lev = np.zeros((2, 6, 144), np.float32)
    for t in range(144):
        lev[t % 12 // 6, t % 6, t] = 1
    colt = col.T.copy()
    levt = lev.transpose(0, 2, 1).copy()
    return [
        m.astype(ml_dtypes.bfloat16)
        for m in (pack, unpack, ret, home, rep, heads, shift, rows, trows, col, lev, colt, levt)
    ]


def mm(a, b):
    return lax.dot_general(a, b, (((1,), (0,)), ((), ())), preferred_element_type=F32)


def mmt(a, b):
    return lax.dot_general(a, b, (((1,), (1,)), ((), ())), preferred_element_type=F32)


def mtm(a, b):
    return lax.dot_general(a, b, (((0,), (0,)), ((), ())), preferred_element_type=F32)


def kernel(
    x_ref, g_ref, gain_ref, wqkv_ref, wproj_ref, table_ref, regions_ref,
    pack_ref, unpack_ref, ret_ref, home_ref, rep_ref, heads_ref, shift_ref, rows_ref, trows_ref,
    col_ref, lev_ref, colt_ref, levt_ref,
    out_x, out_qkv, out_proj, out_gain, out_table,
    xs, gs, zsend, zrecv, osend, orecv, t2, bm,
    main_f, main_s, main_r, xy_f, xy_s, xy_r, z_s, z_r, z_ag, fin,
    tcx_s, tcx_r, tz_s, tz_r, tz_ag, tfin, sq,
    halo_ss, halo_rs, ret_ss, ret_rs, core_ss, core_rs, xy_ss, xy_rs, z_ss, z_rs,
    zag_ss, zag_rs, xyag_ss, xyag_rs, cag_ss, cag_rs,
    tcx_ss, tcx_rs, tz_ss, tz_rs, tzag_ss, tzag_rs, tcag_ss, tcag_rs, sq_ss, sq_rs,
):
    lat = lax.axis_index("lat")
    lon = lax.axis_index("lon")
    nlat, nlon = NLAT, NX * ZLO * 2
    y, z_hi = lat // ZHI, lax.rem(lat, ZHI)
    core = lax.rem(lon, 2)
    chip = lon // 2
    x, z_lo = chip // ZLO, lax.rem(chip, ZLO)
    z = z_hi * ZLO + z_lo
    p = x * NY + y
    cx = x * 2 + core

    def lon_of(x_, z_lo_, core_):
        return (x_ * ZLO + z_lo_) * 2 + core_

    core_peer = (lat, lon_of(x, z_lo, 1 - core))

    def xy_peer(o):
        other = lax.rem(p + o, NXY)
        return other, ((other // NY) * 0 + lax.rem(other, NY) * ZHI + z_hi, lon_of(other // NY, z_lo, core))

    def z_peer(o):
        other = lax.rem(z + o, NZ)
        return other, (y * ZHI + other // ZLO, lon_of(x, lax.rem(other, ZLO), core))

    def cx_peer(o):
        other = lax.rem(cx + o, NCX)
        return other, (lat, lon_of(other // 2, z_lo, lax.rem(other, 2)))

    def zlo_peer(o):
        other = lax.rem(z_lo + o, ZLO)
        return other, (lat, lon_of(x, other, core))

    def lat_peer(o):
        return (lax.rem(lat + o, NLAT), lon)

    before = lambda ah, bh: (lax.rem(lat + nlat - ah, nlat), lax.rem(lon + nlon - bh, nlon))
    after = lambda ah, bh: (lax.rem(lat + ah, nlat), lax.rem(lon + bh, nlon))

    barrier = pltpu.get_barrier_semaphore()

    def greet(device):
        pl.semaphore_signal(barrier, inc=1, device_id=device, device_id_type=MESH)

    greet(core_peer)
    for ah, bh in ((0, 1), (1, 0), (1, 1)):
        greet(before(ah, bh))
        greet(after(ah, bh))

    @pl.loop(1, NXY)
    def _(o):
        greet(xy_peer(o)[1])
        greet(z_peer(o)[1])

    @pl.loop(1, NCX)
    def _(o):
        greet(cx_peer(o)[1])
        greet(lat_peer(o))

    xs[...] = jnp.zeros_like(xs)
    gs[...] = jnp.zeros_like(gs)
    for l in range(2):
        for i in range(6):
            xs[pl.ds((l * 6 + i) * 16, 12), :] = x_ref[l, i]
            gs[pl.ds((l * 6 + i) * 16, 12), :] = g_ref[l, i]
    high = jnp.concatenate([xs[:, 128:192], gs[:, 128:192]], axis=1)
    pieces = mm(pack_ref[0], xs[:, 0:128]) + mm(pack_ref[1], gs[:, 0:128]) + mm(pack_ref[2], high)
    zsend[...] = pieces.astype(BF).reshape(4, 112, 128)
    zrecv[0] = zsend[0]

    pl.semaphore_wait(barrier, 1 + 6 + 2 * (NXY - 1) + 2 * (NCX - 1))

    def remote(src, dst, ss, rs, device):
        return pltpu.make_async_remote_copy(
            src_ref=src, dst_ref=dst, send_sem=ss, recv_sem=rs, device_id=device, device_id_type=MESH
        )

    halo = [
        remote(zsend.at[q], zrecv.at[q], halo_ss.at[q], halo_rs.at[q], before(q // 2, q % 2))
        for q in (1, 2, 3)
    ]
    for c in (halo[2], halo[1], halo[0]):
        c.start()

    t2[...] = jnp.zeros_like(t2)
    for l_s in range(2):
        for a_s in range(6):
            la = l_s * 6 + a_s
            for l_t in range(2):
                off = l_s * 1656 + l_t * 828 + a_s * 138
                t2[pl.ds(la * 6, 6), pl.ds(l_t * 138, 138)] = table_ref[0, :, pl.ds(off, 138)]
    t_all = t2[...]
    t_hi = t_all.astype(BF)
    t_rest = t_all - t_hi.astype(F32)
    t_mid = t_rest.astype(BF)
    t_lo = (t_rest - t_mid.astype(F32)).astype(BF)

    reg_row = jnp.zeros((1, 144), F32)
    reg_col = jnp.zeros((144, 1), F32)
    for l in range(2):
        reg = regions_ref[l].astype(F32).astype(BF)
        reg_row += jnp.sum(mm(reg, col_ref[...]) * lev_ref[l].astype(F32), axis=0, keepdims=True)
        reg_col += jnp.sum(mmt(colt_ref[...], reg) * levt_ref[l].astype(F32), axis=1, keepdims=True)
    same = (reg_row == reg_col).astype(F32).astype(BF)
    for b in range(12):
        sel = shift_ref[b]
        bias = mmt(t_hi, sel) + mmt(t_mid, sel) + mmt(t_lo, sel)
        keep = mm(rep_ref[pl.ds(b * 72, 72), :], same)
        bm[pl.ds(b * 72, 72), :] = jnp.where(keep > 0.5, bias, -1e30)

    for c in halo:
        c.wait_recv()
    zcat = zrecv[...].reshape(448, 128)
    c0 = mm(unpack_ref[0], zcat)
    c1 = mm(unpack_ref[1], zcat)
    c2 = mm(unpack_ref[2], zcat)
    win_x = jnp.concatenate([c0, c2[:, 0:64]], axis=1)
    win_g = jnp.concatenate([c1, c2[:, 64:128]], axis=1).astype(BF)

    gain = gain_ref[...]
    mean = jnp.mean(win_x, axis=-1, keepdims=True)
    centred = win_x - mean
    inv_std = lax.rsqrt(jnp.mean(centred * centred, axis=-1, keepdims=True) + EPS_NORM)
    standard = centred * inv_std
    normed = (standard * gain).astype(BF)
    projected = mm(normed, wqkv_ref[...])
    q = projected[:, 0:192].astype(BF)
    k = projected[:, 192:384].astype(BF)
    v = projected[:, 384:576].astype(BF)
    grad_mixed = mmt(win_g, wproj_ref[...]).astype(BF)

    rep = rep_ref[...]
    heads = heads_ref[...]
    heads_f = heads.astype(F32)
    qm = (mm(rep, q) * heads_f).astype(BF)
    gm = (mm(rep, grad_mixed) * heads_f).astype(BF)
    scores = mmt(qm, k) * SCALE + bm[...]
    top = jnp.max(scores, axis=-1, keepdims=True)
    e = jnp.exp(scores - top)
    probs = e / jnp.sum(e, axis=-1, keepdims=True)
    probs_low = probs.astype(BF)
    grad_probs = mmt(gm, v)
    grad_scores = probs * (grad_probs - jnp.sum(probs * grad_probs, axis=-1, keepdims=True))
    gs_low = grad_scores.astype(BF)
    mixed = mtm(rep, (mm(probs_low, v) * heads_f).astype(BF)).astype(BF)
    gq = mtm(rep, (mm(gs_low, k) * SCALE * heads_f).astype(BF))
    gk = mtm(gs_low, qm) * SCALE
    gv = mtm(probs_low, gm)
    gpi = jnp.concatenate([gq, gk, gv], axis=1).astype(BF)

    normed_pad = mm(normed, rows_ref[...]).astype(BF)
    mixed_pad = mm(mixed, rows_ref[...]).astype(BF)
    g_qkv = mtm(normed_pad, gpi)
    g_proj = mtm(mixed_pad, win_g)
    main_f[0] = g_qkv[:, 0:384]
    main_f[1] = jnp.concatenate([g_qkv[:, 384:576], g_proj], axis=1)
    main_s[...] = main_f[1 - core].astype(BF)
    core_rs_copy = remote(main_s, main_r, core_ss, core_rs, core_peer)
    core_rs_copy.start()

    grad_normed = mmt(gpi, wqkv_ref[...])
    gain_raw = jnp.sum(grad_normed * standard, axis=0, keepdims=True)
    grad_std = grad_normed * gain
    grad_x = inv_std * (
        grad_std
        - jnp.mean(grad_std, axis=-1, keepdims=True)
        - standard * jnp.mean(grad_std * standard, axis=-1, keepdims=True)
    )
    gx_low = grad_x[:, 0:128].astype(BF)
    gx_high = jnp.concatenate([grad_x[:, 128:192], grad_x[:, 128:192]], axis=1).astype(BF)
    lane = lax.broadcasted_iota(jnp.int32, (256, 128), 1)
    back = mm(ret_ref[0], gx_low) + jnp.where(lane < 64, mm(ret_ref[1], gx_high), mm(ret_ref[2], gx_high))
    osend[...] = back.astype(BF).reshape(4, 64, 128)
    orecv[0] = osend[0]
    ret_copies = [
        remote(osend.at[q_], orecv.at[q_], ret_ss.at[q_], ret_rs.at[q_], after(q_ // 2, q_ % 2))
        for q_ in (1, 2, 3)
    ]
    for c in (ret_copies[2], ret_copies[1], ret_copies[0]):
        c.start()

    core_rs_copy.wait_recv()
    half = main_f[core] + main_r[...].astype(F32)
    xy_f[...] = half.reshape(16, 16, 384)
    xy_f[0, 12:13, 0:192] = gain_raw
    xy_s[...] = xy_f[...].astype(BF)

    def xy_copy(o):
        other, device = xy_peer(o)
        return remote(xy_s.at[other], xy_r.at[o - 1], xy_ss.at[o - 1], xy_rs.at[o - 1], device)

    @pl.loop(1, NXY)
    def _(o):
        xy_copy(o).start()

    t_acc = jnp.zeros((72, 384), F32)
    for b in range(12):
        t_acc += mm(gs_low[b * 72:(b + 1) * 72, :], shift_ref[b])
    tcx_s[...] = mm(trows_ref[...], t_acc.astype(BF)).astype(BF).reshape(8, 16, 384)

    def tcx_copy(o):
        other, device = cx_peer(o)
        return remote(tcx_s.at[other], tcx_r.at[o - 1], tcx_ss.at[o - 1], tcx_rs.at[o - 1], device)

    @pl.loop(1, NCX)
    def _(o):
        tcx_copy(o).start()

    @pl.loop(1, NXY)
    def _(o):
        xy_copy(o).wait_recv()

    acc = xy_f[p]
    for o in range(NXY - 1):
        acc += xy_r[o].astype(F32)
    for j in range(NZ):
        z_s[j] = acc[j:j + 1, :]

    def z_copy(o):
        other, device = z_peer(o)
        return remote(z_s.at[other], z_r.at[o - 1], z_ss.at[o - 1], z_rs.at[o - 1], device)

    @pl.loop(1, NZ)
    def _(o):
        z_copy(o).start()

    @pl.loop(1, NCX)
    def _(o):
        tcx_copy(o).wait_recv()

    tacc = tcx_s[cx].astype(F32)
    for o in range(NCX - 1):
        tacc += tcx_r[o].astype(F32)
    for j in range(16):
        tz_s[j] = tacc[j:j + 1, :]

    def tz_copy(o):
        other, device = zlo_peer(o)
        return remote(tz_s.at[pl.ds(other * 2, 2)], tz_r.at[o - 1], tz_ss.at[o - 1], tz_rs.at[o - 1], device)

    @pl.loop(1, ZLO)
    def _(o):
        tz_copy(o).start()

    @pl.loop(1, NZ)
    def _(o):
        z_copy(o).wait_recv()

    row = z_s[z]
    for o in range(NZ - 1):
        row += z_r[o]
    z_ag[z] = row

    def zag_copy(o):
        _, device = z_peer(o)
        return remote(z_ag.at[z], z_ag.at[z], zag_ss.at[o - 1], zag_rs.at[o - 1], device)

    @pl.loop(1, NZ)
    def _(o):
        zag_copy(o).start()

    @pl.loop(1, ZLO)
    def _(o):
        tz_copy(o).wait_recv()

    trow = tz_s[pl.ds(z_lo * 2, 2)]
    for o in range(ZLO - 1):
        trow += tz_r[o]
    tz_ag[pl.ds(z_lo * 2, 2)] = trow

    def tzag_copy(o):
        _, device = zlo_peer(o)
        mine = tz_ag.at[pl.ds(z_lo * 2, 2)]
        return remote(mine, mine, tzag_ss.at[o - 1], tzag_rs.at[o - 1], device)

    @pl.loop(1, ZLO)
    def _(o):
        tzag_copy(o).start()

    @pl.loop(1, NZ)
    def _(o):
        other = lax.rem(z + NZ - o, NZ)
        remote(z_ag.at[other], z_ag.at[other], zag_ss.at[o - 1], zag_rs.at[o - 1], z_peer(o)[1]).wait_recv()

    fin[core, p] = jnp.concatenate([z_ag[j] for j in range(NZ)], axis=0).astype(BF)

    def xyag_copy(o):
        _, device = xy_peer(o)
        return remote(fin.at[core, p], fin.at[core, p], xyag_ss.at[o - 1], xyag_rs.at[o - 1], device)

    @pl.loop(1, NXY)
    def _(o):
        xyag_copy(o).start()

    @pl.loop(1, ZLO)
    def _(o):
        other = lax.rem(z_lo + ZLO - o, ZLO)
        theirs = tz_ag.at[pl.ds(other * 2, 2)]
        remote(theirs, theirs, tzag_ss.at[o - 1], tzag_rs.at[o - 1], zlo_peer(o)[1]).wait_recv()

    tfin[cx] = jnp.concatenate([tz_ag[j] for j in range(16)], axis=0).astype(BF)

    def tcag_copy(o):
        _, device = cx_peer(o)
        return remote(tfin.at[cx], tfin.at[cx], tcag_ss.at[o - 1], tcag_rs.at[o - 1], device)

    @pl.loop(1, NCX)
    def _(o):
        tcag_copy(o).start()

    for c in ret_copies:
        c.wait_recv()
    got = orecv[...].reshape(256, 128)
    h0 = mm(home_ref[0], got)
    h1 = mm(home_ref[1], got)
    h2 = mm(home_ref[2], got)
    grad_in = jnp.concatenate([h0, h1[:, 0:64] + h2[:, 64:128]], axis=1) + gs[...].astype(F32)
    grad_in = grad_in.astype(BF)
    for l in range(2):
        for i in range(6):
            r0 = (l * 6 + i) * 16
            out_x[l, i] = grad_in[r0:r0 + 12, :]

    @pl.loop(1, NXY)
    def _(o):
        other = lax.rem(p + NXY - o, NXY)
        slot = fin.at[core, other]
        remote(slot, slot, xyag_ss.at[o - 1], xyag_rs.at[o - 1], xy_peer(o)[1]).wait_recv()

    cag = remote(fin.at[core], fin.at[core], cag_ss, cag_rs, core_peer)
    cag.start()

    @pl.loop(1, NCX)
    def _(o):
        other = lax.rem(cx + NCX - o, NCX)
        slot = tfin.at[other]
        remote(slot, slot, tcag_ss.at[o - 1], tcag_rs.at[o - 1], cx_peer(o)[1]).wait_recv()

    band = mtm(trows_ref[...], tfin[...].reshape(128, 384))
    squares = jnp.sum(jnp.sum(band * band, axis=1, keepdims=True), axis=0, keepdims=True)
    sq[lat] = jnp.broadcast_to(squares, (1, 128))

    def sq_copy(o):
        return remote(sq.at[lat], sq.at[lat], sq_ss.at[o - 1], sq_rs.at[o - 1], lat_peer(o))

    @pl.loop(1, NLAT)
    def _(o):
        sq_copy(o).start()

    other_half = fin.at[1 - core]
    remote(other_half, other_half, cag_ss, cag_rs, core_peer).wait_recv()
    whole = jnp.concatenate([fin[0].reshape(256, 384), fin[1].reshape(256, 384)], axis=1)
    whole = mm(rows_ref[...], whole)
    w_q, w_p = whole[:, 0:576], whole[:, 576:768]
    w_g = fin[0, 0, 12:13, 0:192].astype(F32) + fin[1, 0, 12:13, 0:192].astype(F32)

    def rescaled(value, entries):
        total = jnp.sum(jnp.sum(value * value, axis=1, keepdims=True), axis=0, keepdims=True)
        return value / jnp.sqrt(total / entries + EPS_RMS)

    out_qkv[...] = rescaled(w_q, 192 * 576)
    out_proj[...] = rescaled(w_p, 192 * 192)
    out_gain[...] = rescaled(w_g, 192)

    @pl.loop(1, NLAT)
    def _(o):
        slot = sq.at[lax.rem(lat + NLAT - o, NLAT)]
        remote(slot, slot, sq_ss.at[o - 1], sq_rs.at[o - 1], lat_peer(o)).wait_recv()

    total = sq[0]
    for j in range(1, NLAT):
        total += sq[j]
    band = band / jnp.sqrt(total[:, 0:1] / (NLAT * 6 * 3312) + EPS_RMS)
    for l_s in range(2):
        for a_s in range(6):
            la = l_s * 6 + a_s
            for l_t in range(2):
                off = l_s * 1656 + l_t * 828 + a_s * 138
                out_table[0, :, pl.ds(off, 138)] = band[la * 6:la * 6 + 6, l_t * 138:l_t * 138 + 138]

    for c in halo + ret_copies + [core_rs_copy, cag]:
        c.wait_send()

    @pl.loop(1, NXY)
    def _(o):
        xy_copy(o).wait_send()
        z_copy(o).wait_send()
        zag_copy(o).wait_send()
        xyag_copy(o).wait_send()

    @pl.loop(1, NCX)
    def _(o):
        tcx_copy(o).wait_send()
        tz_copy(o).wait_send()
        tzag_copy(o).wait_send()
        tcag_copy(o).wait_send()
        sq_copy(o).wait_send()


def on_device(activations, cotangent, gain, w_qkv, w_proj, bias_table, regions):
    consts = [jnp.asarray(m) for m in tables()]
    vmem = pl.BlockSpec(memory_space=pltpu.VMEM)
    dma = pltpu.SemaphoreType.DMA
    scratch = [
        pltpu.VMEM((192, 192), BF), pltpu.VMEM((192, 192), BF),
        pltpu.VMEM((4, 112, 128), BF), pltpu.VMEM((4, 112, 128), BF),
        pltpu.VMEM((4, 64, 128), BF), pltpu.VMEM((4, 64, 128), BF),
        pltpu.VMEM((72, 384), F32), pltpu.VMEM((864, 144), F32),
        pltpu.VMEM((2, 256, 384), F32), pltpu.VMEM((256, 384), BF), pltpu.VMEM((256, 384), BF),
        pltpu.VMEM((16, 16, 384), F32), pltpu.VMEM((16, 16, 384), BF), pltpu.VMEM((15, 16, 384), BF),
        pltpu.VMEM((16, 1, 384), F32), pltpu.VMEM((15, 1, 384), F32), pltpu.VMEM((16, 1, 384), F32),
        pltpu.VMEM((2, 16, 16, 384), BF),
        pltpu.VMEM((8, 16, 384), BF), pltpu.VMEM((7, 16, 384), BF),
        pltpu.VMEM((16, 1, 384), F32), pltpu.VMEM((7, 2, 1, 384), F32), pltpu.VMEM((16, 1, 384), F32),
        pltpu.VMEM((8, 16, 384), BF), pltpu.VMEM((8, 1, 128), F32),
        dma((4,)), dma((4,)), dma((4,)), dma((4,)), dma, dma,
        dma((15,)), dma((15,)), dma((15,)), dma((15,)),
        dma((15,)), dma((15,)), dma((15,)), dma((15,)), dma, dma,
        dma((7,)), dma((7,)), dma((7,)), dma((7,)),
        dma((7,)), dma((7,)), dma((7,)), dma((7,)), dma((7,)), dma((7,)),
    ]
    outs = pl.pallas_call(
        kernel,
        out_shape=(
            jax.ShapeDtypeStruct((2, 6, 12, 192), BF),
            jax.ShapeDtypeStruct((192, 576), F32),
            jax.ShapeDtypeStruct((192, 192), F32),
            jax.ShapeDtypeStruct((1, 192), F32),
            jax.ShapeDtypeStruct((1, 6, 3312), F32),
        ),
        in_specs=[vmem] * 20,
        out_specs=(vmem,) * 5,
        scratch_shapes=scratch,
        compiler_params=pltpu.CompilerParams(
            collective_id=0, has_side_effects=True, vmem_limit_bytes=48 * 1024 * 1024
        ),
        name="swin_backward",
    )(activations, cotangent, gain.reshape(1, 192), w_qkv, w_proj, bias_table, regions, *consts)
    return outs[0], outs[1], outs[2], outs[3].reshape(192), outs[4]


def solution(mesh):
    in_specs = (
        P(None, "lat", "lon", None),
        P(None, "lat", "lon", None),
        P(),
        P(),
        P(),
        P("lat", None, None),
        P(None, "lat", "lon"),
    )
    out_specs = (P(None, "lat", "lon", None), P(), P(), P(), P("lat", None, None))
    return jax.shard_map(
        on_device, mesh=mesh, in_specs=in_specs, out_specs=out_specs, check_vma=False
    )
```

```python
import functools

import jax
import jax.numpy as jnp
import ml_dtypes
import numpy as np
from jax import lax
from jax.experimental import pallas as pl
from jax.experimental.pallas import tpu as pltpu
from jax.sharding import PartitionSpec as P

F32 = jnp.float32
BF = jnp.bfloat16
MESH = pl.DeviceIdType.MESH

EPS_NORM = 1e-05
EPS_RMS = 1e-06
SCALE = 32.0 ** -0.5

NX, NY, ZHI, ZLO = 4, 4, 2, 8
NXY = NX * NY
NLAT = NY * ZHI
NCX = NX * 2


def tables():
    tok = np.arange(144)
    ta, tb, tl = tok // 24, tok // 2 % 12, 1 - tok % 2
    la = tl * 6 + ta
    row = np.arange(864)
    rb, rla, rh = row // 72, row // 6 % 12, row % 6
    rep = (rb[:, None] == tb[None, :]) & (rla[:, None] == la[None, :])
    heads = rh[:, None] == np.arange(192)[None, :] // 32
    shift = np.zeros((12, 144, 384), np.float32)
    for bs in range(12):
        shift[bs, tok, la * 23 + tb - bs + 11] = 1
    rows = np.zeros((192, 256), np.float32)
    chan = np.arange(192)
    rows[chan, chan // 12 * 16 + chan % 12] = 1
    trows = np.zeros((128, 72), np.float32)
    r = np.arange(72)
    trows[r // 9 * 16 + r % 9, r] = 1
    col = tb[None, :] == np.arange(12)[:, None]
    lev = (ta[None, None, :] == np.arange(6)[:, None, None]) & (tl[None, None, :] == np.arange(2)[None, :, None])
    colt = col.T
    levt = lev.transpose(0, 2, 1)
    return [
        np.ascontiguousarray(m).astype(ml_dtypes.bfloat16)
        for m in (rep, heads, shift, rows, trows, col, lev, colt, levt)
    ]


def mm(a, b):
    return lax.dot_general(a, b, (((1,), (0,)), ((), ())), preferred_element_type=F32)


def mmt(a, b):
    return lax.dot_general(a, b, (((1,), (1,)), ((), ())), preferred_element_type=F32)


def mtm(a, b):
    return lax.dot_general(a, b, (((0,), (0,)), ((), ())), preferred_element_type=F32)


def kernel(
    x_hbm, g_hbm, gain_hbm, wqkv_hbm, wproj_hbm, table_hbm, regions_hbm,
    rep_hbm, heads_hbm, shift_hbm, rows_hbm, trows_hbm, col_hbm, lev_hbm, colt_hbm, levt_hbm,
    out_x, out_qkv, out_proj, out_gain, out_table,
    gain_ref, wqkv_ref, wproj_ref, table_ref, regions_ref,
    rep_ref, heads_ref, shift_ref, rows_ref, trows_ref, col_ref, lev_ref, colt_ref, levt_ref,
    own_g, wx, wg, gxw, orecv, xs, gs, gx, t1, t2, bm,
    main_f, main_s, main_r, xy_f, xy_s, xy_r, za, zb, piece, fin,
    tcx_s, tcx_r, ta, tb, tfin, sq,
    load_sem, quarter_sem, halo_ss, halo_rs, ret_ss, ret_rs, core_ss, core_rs, xy_ss, xy_rs, za_ss, za_rs, zb_ss, zb_rs,
    xyag_ss, xyag_rs, cag_ss, cag_rs,
    tcx_ss, tcx_rs, ta_ss, ta_rs, tb_ss, tb_rs, tcag_ss, tcag_rs, sq_ss, sq_rs,
):
    lat = lax.axis_index("lat")
    lon = lax.axis_index("lon")
    nlat, nlon = NLAT, NX * ZLO * 2
    y, z_hi = lat // ZHI, lax.rem(lat, ZHI)
    core = lax.rem(lon, 2)
    chip = lon // 2
    x, z_lo = chip // ZLO, lax.rem(chip, ZLO)
    zq, zr = z_hi * 2 + z_lo // 4, lax.rem(z_lo, 4)
    zhalf = z_lo // 4
    p = x * NY + y
    cx = x * 2 + core

    def lon_of(x_, z_lo_, core_):
        return (x_ * ZLO + z_lo_) * 2 + core_

    core_peer = (lat, lon_of(x, z_lo, 1 - core))

    def xy_peer(o):
        other = lax.rem(p + o, NXY)
        return other, ((other // NY) * 0 + lax.rem(other, NY) * ZHI + z_hi, lon_of(other // NY, z_lo, core))

    def zr_peer(o):
        return (lat, lon_of(x, zhalf * 4 + lax.rem(zr + o, 4), core))

    def zq_peer(o):
        other = lax.rem(zq + o, 4)
        return (y * ZHI + other // 2, lon_of(x, lax.rem(other, 2) * 4 + zr, core))

    def cx_peer(o):
        other = lax.rem(cx + o, NCX)
        return other, (lat, lon_of(other // 2, z_lo, lax.rem(other, 2)))

    far_half = (lat, lon_of(x, lax.rem(z_lo + 4, ZLO), core))
    far_hi = (y * ZHI + 1 - z_hi, lon)

    before = lambda ah, bh: (lax.rem(lat + nlat - ah, nlat), lax.rem(lon + nlon - bh, nlon))
    after = lambda ah, bh: (lax.rem(lat + ah, nlat), lax.rem(lon + bh, nlon))

    barrier = pltpu.get_barrier_semaphore()

    def greet(device):
        pl.semaphore_signal(barrier, inc=1, device_id=device, device_id_type=MESH)

    greet(core_peer)
    for ah, bh in ((0, 1), (1, 0), (1, 1)):
        greet(before(ah, bh))
        greet(after(ah, bh))

    @pl.loop(1, NXY)
    def _(o):
        greet(xy_peer(o)[1])

    for o in range(1, 4):
        greet(zr_peer(o))
        greet(zq_peer(o))
        greet((lat, lon_of(lax.rem(x + o, NX), z_lo, 1 - core)))

    pairs = (
        (regions_hbm, regions_ref), (col_hbm, col_ref), (lev_hbm, lev_ref), (colt_hbm, colt_ref), (levt_hbm, levt_ref),
        (rep_hbm, rep_ref), (table_hbm, table_ref), (shift_hbm, shift_ref), (heads_hbm, heads_ref),
        (wqkv_hbm, wqkv_ref), (wproj_hbm, wproj_ref), (gain_hbm, gain_ref), (rows_hbm, rows_ref),
        (trows_hbm, trows_ref), (g_hbm, own_g),
    )
    loads = [pltpu.make_async_copy(src, dst, load_sem.at[n]) for n, (src, dst) in enumerate(pairs)]
    for c in loads:
        c.start()
    quarter = [
        pltpu.make_async_copy(src.at[pl.ds(3, 3), pl.ds(6, 6)], dst.at[pl.ds(0, 3), pl.ds(0, 6)], quarter_sem.at[n])
        for n, (src, dst) in enumerate(((x_hbm, wx), (g_hbm, wg)))
    ]
    for c in quarter:
        c.start()

    pl.semaphore_wait(barrier, 1 + 6 + (NXY - 1) + 9)

    def remote(src, dst, ss, rs, device):
        return pltpu.make_async_remote_copy(
            src_ref=src, dst_ref=dst, send_sem=ss, recv_sem=rs, device_id=device, device_id_type=MESH
        )

    def here(ah, bh):
        return pl.ds(3 - 3 * ah, 3), pl.ds(6 - 6 * bh, 6)

    def there(ah, bh):
        return pl.ds(3 * ah, 3), pl.ds(6 * bh, 6)

    halo = []
    for ah, bh in ((1, 1), (1, 0), (0, 1)):
        for n, (src, dst) in enumerate(((x_hbm, wx), (g_hbm, wg))):
            at = (ah * 2 + bh) * 2 + n
            halo.append(remote(
                src.at[here(ah, bh)], dst.at[there(ah, bh)], halo_ss.at[at], halo_rs.at[at], before(ah, bh)
            ))
    for c in halo:
        c.start()

    for c in loads:
        c.wait()
    t2[...] = jnp.zeros_like(t2)
    for h in range(6):
        t1[h:h + 1, :] = table_ref[h]
    for l_s in range(2):
        for a_s in range(6):
            la = l_s * 6 + a_s
            for l_t in range(2):
                off = l_s * 1656 + l_t * 828 + a_s * 138
                t2[pl.ds(la * 6, 6), pl.ds(l_t * 138, 138)] = t1[:, pl.ds(off, 138)]
    t_all = t2[...]
    t_hi = t_all.astype(BF)
    t_rest = t_all - t_hi.astype(F32)
    t_mid = t_rest.astype(BF)
    t_lo = (t_rest - t_mid.astype(F32)).astype(BF)

    reg_row = jnp.zeros((1, 144), F32)
    reg_col = jnp.zeros((144, 1), F32)
    for i in range(6):
        reg = regions_ref[i].astype(F32).astype(BF)
        reg_row += jnp.sum(mm(reg, col_ref[...]) * lev_ref[i].astype(F32), axis=0, keepdims=True)
        reg_col += jnp.sum(mmt(colt_ref[...], reg) * levt_ref[i].astype(F32), axis=1, keepdims=True)
    same = (reg_row == reg_col).astype(F32).astype(BF)
    for b in range(12):
        sel = shift_ref[b]
        bias = mmt(t_hi, sel) + mmt(t_mid, sel) + mmt(t_lo, sel)
        keep = mm(rep_ref[pl.ds(b * 72, 72), :], same)
        bm[pl.ds(b * 72, 72), :] = jnp.where(keep > 0.5, bias, -1e30)

    for c in quarter:
        c.wait()
    for c in halo:
        c.wait_recv()
    for n in range(72):
        xs[2 * n:2 * n + 2, :] = wx[n // 12, n % 12]
        gs[2 * n:2 * n + 2, :] = wg[n // 12, n % 12]
    win_x = xs[...].astype(F32)
    win_g = gs[...]

    gain = gain_ref[...]
    mean = jnp.mean(win_x, axis=-1, keepdims=True)
    centred = win_x - mean
    inv_std = lax.rsqrt(jnp.mean(centred * centred, axis=-1, keepdims=True) + EPS_NORM)
    standard = centred * inv_std
    normed = (standard * gain).astype(BF)
    projected = mm(normed, wqkv_ref[...])
    q = projected[:, 0:192].astype(BF)
    k = projected[:, 192:384].astype(BF)
    v = projected[:, 384:576].astype(BF)
    grad_mixed = mmt(win_g, wproj_ref[...]).astype(BF)

    rep = rep_ref[...]
    heads = heads_ref[...]
    heads_f = heads.astype(F32)
    qm = (mm(rep, q) * heads_f).astype(BF)
    gm = (mm(rep, grad_mixed) * heads_f).astype(BF)
    scores = mmt(qm, k) * SCALE + bm[...]
    top = jnp.max(scores, axis=-1, keepdims=True)
    e = jnp.exp(scores - top)
    probs = e / jnp.sum(e, axis=-1, keepdims=True)
    probs_low = probs.astype(BF)
    grad_probs = mmt(gm, v)
    grad_scores = probs * (grad_probs - jnp.sum(probs * grad_probs, axis=-1, keepdims=True))
    gs_low = grad_scores.astype(BF)
    mixed = mtm(rep, (mm(probs_low, v) * heads_f).astype(BF)).astype(BF)
    gq = mtm(rep, (mm(gs_low, k) * SCALE * heads_f).astype(BF))
    gk = mtm(gs_low, qm) * SCALE
    gv = mtm(probs_low, gm)
    gpi = jnp.concatenate([gq, gk, gv], axis=1).astype(BF)

    normed_pad = mm(normed, rows_ref[...]).astype(BF)
    mixed_pad = mm(mixed, rows_ref[...]).astype(BF)
    g_qkv = mtm(normed_pad, gpi)
    g_proj = mtm(mixed_pad, win_g)
    main_f[0] = g_qkv[:, 0:384]
    main_f[1] = jnp.concatenate([g_qkv[:, 384:576], g_proj], axis=1)
    main_s[...] = main_f[1 - core].astype(BF)
    core_rs_copy = remote(main_s, main_r, core_ss, core_rs, core_peer)
    core_rs_copy.start()

    grad_normed = mmt(gpi, wqkv_ref[...])
    gain_raw = jnp.sum(grad_normed * standard, axis=0, keepdims=True)
    grad_std = grad_normed * gain
    grad_x = inv_std * (
        grad_std
        - jnp.mean(grad_std, axis=-1, keepdims=True)
        - standard * jnp.mean(grad_std * standard, axis=-1, keepdims=True)
    )
    gx[...] = grad_x.astype(BF)
    for n in range(72):
        gxw[n // 12, n % 12] = gx[2 * n:2 * n + 2, :]
    ret_copies = [
        remote(gxw.at[there(ah, bh)], orecv.at[here(ah, bh)], ret_ss.at[ah * 2 + bh], ret_rs.at[ah * 2 + bh], after(ah, bh))
        for ah, bh in ((1, 1), (1, 0), (0, 1))
    ]
    for c in ret_copies:
        c.start()
    orecv[here(0, 0)] = gxw[there(0, 0)]

    core_rs_copy.wait_recv()
    half = main_f[core] + main_r[...].astype(F32)
    xy_f[...] = half.reshape(16, 16, 384)
    xy_f[0, 12:13, 0:192] = gain_raw
    xy_s[...] = xy_f[...].astype(BF)

    def xy_copy(o):
        other, device = xy_peer(o)
        return remote(xy_s.at[other], xy_r.at[o - 1], xy_ss.at[o - 1], xy_rs.at[o - 1], device)

    @pl.loop(1, NXY)
    def _(o):
        xy_copy(o).start()

    t_acc = jnp.zeros((72, 384), F32)
    for b in range(12):
        t_acc += mm(gs_low[b * 72:(b + 1) * 72, :], shift_ref[b])
    tcx_s[...] = mm(trows_ref[...], t_acc.astype(BF)).astype(BF).reshape(8, 16, 384)

    def tcx_copy(o):
        other, device = cx_peer(o)
        return remote(tcx_s.at[other], tcx_r.at[o - 1], tcx_ss.at[o - 1], tcx_rs.at[o - 1], device)

    @pl.loop(1, NCX)
    def _(o):
        tcx_copy(o).start()

    for c in halo + [core_rs_copy]:
        c.wait_send()

    @pl.loop(1, NCX)
    def _(o):
        tcx_copy(o).wait_recv()

    tacc = tcx_s[cx].astype(F32)
    for o in range(NCX - 1):
        tacc += tcx_r[o].astype(F32)
    ta[zr] = tacc.astype(BF)

    def spread(buf, at, ss, rs, peer, n):
        out = [remote(buf.at[at], buf.at[at], ss.at[o - 1], rs.at[o - 1], peer(o)) for o in range(1, n)]
        into = []
        for o in range(1, n):
            slot = buf.at[lax.rem(at + n - o, n)]
            into.append(remote(slot, slot, ss.at[o - 1], rs.at[o - 1], peer(o)))
        return out, into

    ta_out, ta_in = spread(ta, zr, ta_ss, ta_rs, zr_peer, 4)
    for c in ta_out:
        c.start()

    @pl.loop(1, NXY)
    def _(o):
        xy_copy(o).wait_recv()

    acc = xy_f[p]
    for o in range(NXY - 1):
        acc += xy_r[o].astype(F32)
    za[zr] = acc.astype(BF)
    za_out, za_in = spread(za, zr, za_ss, za_rs, zr_peer, 4)
    for c in za_out:
        c.start()

    for c in ta_in:
        c.wait_recv()
    tsum = ta[0].astype(F32)
    for j in range(1, 4):
        tsum += ta[j].astype(F32)
    tb[zhalf] = tsum.astype(BF)
    tb_out, tb_in = spread(tb, zhalf, tb_ss, tb_rs, lambda o: far_half, 2)
    tb_out[0].start()

    for c in za_in:
        c.wait_recv()
    acc = za[0].astype(F32)
    for j in range(1, 4):
        acc += za[j].astype(F32)
    zb[zq] = acc.astype(BF)
    zb_out, zb_in = spread(zb, zq, zb_ss, zb_rs, zq_peer, 4)
    for c in zb_out:
        c.start()

    tb_in[0].wait_recv()
    tpiece = tb[0].astype(F32) + tb[1].astype(F32)
    tpiece_low = tpiece.astype(BF)
    tpiece = tpiece_low.astype(F32)
    squares = jnp.sum(jnp.sum(tpiece * tpiece, axis=1, keepdims=True), axis=0, keepdims=True)
    sq[z_hi] = jnp.broadcast_to(squares, (1, 128))
    sq_out, sq_in = spread(sq, z_hi, sq_ss, sq_rs, lambda o: far_hi, 2)
    sq_out[0].start()
    tfin[cx] = tpiece_low

    def tcag_copy(o):
        _, device = cx_peer(o)
        return remote(tfin.at[cx], tfin.at[cx], tcag_ss.at[o - 1], tcag_rs.at[o - 1], device)

    @pl.loop(1, NCX)
    def _(o):
        tcag_copy(o).start()

    for c in ret_copies:
        c.wait()
    out_x[...] = (own_g[...].astype(F32) + orecv[...].astype(F32)).astype(BF)

    @pl.loop(1, NXY)
    def _(o):
        xy_copy(o).wait_send()

    @pl.loop(1, NCX)
    def _(o):
        tcx_copy(o).wait_send()

    for c in ta_out + za_out + tb_out:
        c.wait_send()

    for c in zb_in:
        c.wait_recv()
    acc = zb[0].astype(F32)
    for j in range(1, 4):
        acc += zb[j].astype(F32)
    piece[...] = acc
    sq_in[0].wait_recv()
    both = sq[0] + sq[1]
    both_hi = both.astype(BF).astype(F32)
    both_mid = (both - both_hi).astype(BF).astype(F32)
    both_lo = both - both_hi - both_mid
    lane = lax.broadcasted_iota(jnp.int32, (1, 128), 1)
    piece[13:14, 0:128] = jnp.where(
        lane == 0, both_hi, jnp.where(lane == 1, both_mid, jnp.where(lane == 2, both_lo, 0.0))
    )
    fin[core, p] = piece[...].astype(BF)

    def xyag_copy(o):
        _, device = xy_peer(o)
        return remote(fin.at[core, p], fin.at[core, p], xyag_ss.at[o - 1], xyag_rs.at[o - 1], device)

    @pl.loop(1, NXY)
    def _(o):
        xyag_copy(o).start()

    @pl.loop(1, NCX)
    def _(o):
        other = lax.rem(cx + NCX - o, NCX)
        slot = tfin.at[other]
        remote(slot, slot, tcag_ss.at[o - 1], tcag_rs.at[o - 1], cx_peer(o)[1]).wait_recv()

    band = mtm(trows_ref[...], tfin[...].reshape(128, 384))

    @pl.loop(1, NCX)
    def _(o):
        tcag_copy(o).wait_send()

    for c in zb_out + sq_out:
        c.wait_send()

    @pl.loop(1, NXY)
    def _(o):
        other = lax.rem(p + NXY - o, NXY)
        slot = fin.at[core, other]
        remote(slot, slot, xyag_ss.at[o - 1], xyag_rs.at[o - 1], xy_peer(o)[1]).wait_recv()

    cag = remote(fin.at[core], fin.at[core], cag_ss, cag_rs, core_peer)
    cag.start()

    @pl.loop(1, NXY)
    def _(o):
        xyag_copy(o).wait_send()

    other_half = fin.at[1 - core]
    remote(other_half, other_half, cag_ss, cag_rs, core_peer).wait_recv()
    whole = jnp.concatenate([fin[0].reshape(256, 384), fin[1].reshape(256, 384)], axis=1)
    whole = mm(rows_ref[...], whole)
    w_q, w_p = whole[:, 0:576], whole[:, 576:768]
    w_g = fin[0, 0, 12:13, 0:192].astype(F32) + fin[1, 0, 12:13, 0:192].astype(F32)

    def rescaled(value, entries):
        total = jnp.sum(jnp.sum(value * value, axis=1, keepdims=True), axis=0, keepdims=True)
        return value / jnp.sqrt(total / entries + EPS_RMS)

    out_qkv[...] = rescaled(w_q, 192 * 576)
    out_proj[...] = rescaled(w_p, 192 * 192)
    out_gain[...] = rescaled(w_g, 192)

    shares = jnp.zeros((1, 128), F32)
    for c in range(2):
        for j in range(NXY):
            shares += fin[c, j, 13:14, 0:128].astype(F32)
    total = jnp.sum(shares, axis=1, keepdims=True)
    band = band / jnp.sqrt(total / (NLAT * 6 * 3312) + EPS_RMS)
    for l_s in range(2):
        for a_s in range(6):
            la = l_s * 6 + a_s
            for l_t in range(2):
                off = l_s * 1656 + l_t * 828 + a_s * 138
                t1[:, pl.ds(off, 138)] = band[la * 6:la * 6 + 6, l_t * 138:l_t * 138 + 138]
    for h in range(6):
        out_table[h] = t1[h:h + 1, :]
    cag.wait_send()


def hand_over(*refs):
    sem = refs[-1]
    n = (len(refs) - 1) // 2
    copies = [pltpu.make_async_copy(refs[i], refs[n + i], sem.at[i]) for i in range(n)]
    for c in copies:
        c.start()
    for c in copies:
        c.wait()


def on_device(activations, cotangent, gain, w_qkv, w_proj, bias_table, regions):
    consts = [jnp.asarray(m) for m in tables()]
    vmem = pl.BlockSpec(memory_space=pltpu.VMEM)
    hbm = pl.BlockSpec(memory_space=pltpu.HBM)
    dma = pltpu.SemaphoreType.DMA
    operands = [
        activations.transpose(1, 2, 0, 3), cotangent.transpose(1, 2, 0, 3), gain.reshape(1, 192), w_qkv, w_proj,
        bias_table.transpose(1, 0, 2), regions.transpose(1, 0, 2), *consts,
    ]
    scratch = [pltpu.VMEM(o.shape, o.dtype) for o in operands[2:]] + [
        pltpu.VMEM((6, 12, 2, 192), BF), pltpu.VMEM((6, 12, 2, 192), BF), pltpu.VMEM((6, 12, 2, 192), BF),
        pltpu.VMEM((6, 12, 2, 192), BF), pltpu.VMEM((6, 12, 2, 192), BF),
        pltpu.VMEM((144, 192), BF), pltpu.VMEM((144, 192), BF), pltpu.VMEM((144, 192), BF),
        pltpu.VMEM((6, 3312), F32), pltpu.VMEM((72, 384), F32), pltpu.VMEM((864, 144), F32),
        pltpu.VMEM((2, 256, 384), F32), pltpu.VMEM((256, 384), BF), pltpu.VMEM((256, 384), BF),
        pltpu.VMEM((16, 16, 384), F32), pltpu.VMEM((16, 16, 384), BF), pltpu.VMEM((15, 16, 384), BF),
        pltpu.VMEM((4, 16, 384), BF), pltpu.VMEM((4, 16, 384), BF), pltpu.VMEM((16, 384), F32),
        pltpu.VMEM((2, 16, 16, 384), BF),
        pltpu.VMEM((8, 16, 384), BF), pltpu.VMEM((7, 16, 384), BF),
        pltpu.VMEM((4, 16, 384), BF), pltpu.VMEM((2, 16, 384), BF),
        pltpu.VMEM((8, 16, 384), BF), pltpu.VMEM((2, 1, 128), F32),
        dma((15,)), dma((2,)), dma((8,)), dma((8,)), dma((4,)), dma((4,)), dma, dma,
        dma((15,)), dma((15,)), dma((3,)), dma((3,)), dma((3,)), dma((3,)),
        dma((15,)), dma((15,)), dma, dma,
        dma((7,)), dma((7,)), dma((3,)), dma((3,)), dma((1,)), dma((1,)), dma((7,)), dma((7,)), dma((1,)), dma((1,)),
    ]
    shapes = (
        jax.ShapeDtypeStruct((6, 12, 2, 192), BF),
        jax.ShapeDtypeStruct((192, 576), F32),
        jax.ShapeDtypeStruct((192, 192), F32),
        jax.ShapeDtypeStruct((1, 192), F32),
        jax.ShapeDtypeStruct((6, 1, 3312), F32),
    )
    outs = pl.pallas_call(
        kernel,
        out_shape=shapes,
        in_specs=[hbm] * len(operands),
        out_specs=(vmem,) * 5,
        scratch_shapes=scratch,
        compiler_params=pltpu.CompilerParams(
            collective_id=0, has_side_effects=True, vmem_limit_bytes=40 * 1024 * 1024
        ),
        name="swin_backward",
    )(*[pltpu.with_memory_space_constraint(o, pltpu.HBM) for o in operands])
    outs = pl.pallas_call(
        hand_over,
        out_shape=shapes,
        in_specs=[vmem] * 5,
        out_specs=(hbm,) * 5,
        scratch_shapes=[dma((5,))],
        compiler_params=pltpu.CompilerParams(vmem_limit_bytes=32 * 1024 * 1024),
        name="hand_over",
    )(*outs)
    return outs[0].transpose(2, 0, 1, 3), outs[1], outs[2], outs[3].reshape(192), outs[4].transpose(1, 0, 2)


def solution(mesh):
    in_specs = (
        P(None, "lat", "lon", None),
        P(None, "lat", "lon", None),
        P(),
        P(),
        P(),
        P("lat", None, None),
        P(None, "lat", "lon"),
    )
    out_specs = (P(None, "lat", "lon", None), P(), P(), P(), P("lat", None, None))
    return jax.shard_map(
        on_device, mesh=mesh, in_specs=in_specs, out_specs=out_specs, check_vma=False
    )
```

```python
import functools

import jax
import jax.numpy as jnp
import ml_dtypes
import numpy as np
from jax import lax
from jax.experimental import pallas as pl
from jax.experimental.pallas import tpu as pltpu
from jax.sharding import PartitionSpec as P

F32 = jnp.float32
BF = jnp.bfloat16
MESH = pl.DeviceIdType.MESH

EPS_NORM = 1e-05
EPS_RMS = 1e-06
SCALE = 32.0 ** -0.5

NX, NY, ZHI, ZLO = 4, 4, 2, 8
NXY = NX * NY
NLAT = NY * ZHI
NCX = NX * 2


def tables():
    tok = np.arange(144)
    ta, tb, tl = tok // 24, tok // 2 % 12, 1 - tok % 2
    la = tl * 6 + ta
    row = np.arange(864)
    rb, rla, rh = row // 72, row // 6 % 12, row % 6
    rep = (rb[:, None] == tb[None, :]) & (rla[:, None] == la[None, :])
    heads = rh[:, None] == np.arange(192)[None, :] // 32
    shift = np.zeros((12, 144, 384), np.float32)
    for bs in range(12):
        shift[bs, tok, la * 23 + tb - bs + 11] = 1
    rows = np.zeros((192, 256), np.float32)
    chan = np.arange(192)
    rows[chan, chan // 12 * 16 + chan % 12] = 1
    trows = np.zeros((128, 72), np.float32)
    r = np.arange(72)
    trows[r // 9 * 16 + r % 9, r] = 1
    col = tb[None, :] == np.arange(12)[:, None]
    lev = (ta[None, None, :] == np.arange(6)[:, None, None]) & (tl[None, None, :] == np.arange(2)[None, :, None])
    return [
        np.ascontiguousarray(m).astype(ml_dtypes.bfloat16)
        for m in (rep, heads, shift, rows, trows, col, lev)
    ]


def mm(a, b):
    return lax.dot_general(a, b, (((1,), (0,)), ((), ())), preferred_element_type=F32)


def mmt(a, b):
    return lax.dot_general(a, b, (((1,), (1,)), ((), ())), preferred_element_type=F32)


def mtm(a, b):
    return lax.dot_general(a, b, (((0,), (0,)), ((), ())), preferred_element_type=F32)


def kernel(
    x_hbm, g_hbm, gain_hbm, wqkv_hbm, wproj_hbm, table_hbm, regions_hbm,
    rep_hbm, heads_hbm, shift_hbm, rows_hbm, trows_hbm, col_hbm, lev_hbm,
    out_x, out_qkv, out_proj, out_gain, out_table,
    gain_ref, wqkv_ref, wproj_ref, table_ref, regions_ref,
    rep_ref, heads_ref, shift_ref, rows_ref, trows_ref, col_ref, lev_ref,
    own_x, own_g, reg_s, reg_r, wx, wg, gxw, orecv, xs, gs, gx, t1, t2, bm,
    main_f, main_s, main_r, xy_f, xy_s, xy_r, za, zb, piece, fin,
    tcx_s, tcx_r, ta, tb, tfin, sq,
    load_sem, reg_ss, reg_rs, halo_ss, halo_rs, ret_ss, ret_rs, core_ss, core_rs, xy_ss, xy_rs, za_ss, za_rs, zb_ss, zb_rs,
    xyag_ss, xyag_rs, cag_ss, cag_rs,
    tcx_ss, tcx_rs, ta_ss, ta_rs, tb_ss, tb_rs, tcag_ss, tcag_rs, sq_ss, sq_rs,
):
    lat = lax.axis_index("lat")
    lon = lax.axis_index("lon")
    nlat, nlon = NLAT, NX * ZLO * 2
    y, z_hi = lat // ZHI, lax.rem(lat, ZHI)
    core = lax.rem(lon, 2)
    chip = lon // 2
    x, z_lo = chip // ZLO, lax.rem(chip, ZLO)
    zq, zr = z_hi * 2 + z_lo // 4, lax.rem(z_lo, 4)
    zhalf = z_lo // 4
    p = x * NY + y
    cx = x * 2 + core

    def lon_of(x_, z_lo_, core_):
        return (x_ * ZLO + z_lo_) * 2 + core_

    core_peer = (lat, lon_of(x, z_lo, 1 - core))

    def xy_peer(o):
        other = lax.rem(p + o, NXY)
        return other, ((other // NY) * 0 + lax.rem(other, NY) * ZHI + z_hi, lon_of(other // NY, z_lo, core))

    def zr_peer(o):
        return (lat, lon_of(x, zhalf * 4 + lax.rem(zr + o, 4), core))

    def zq_peer(o):
        other = lax.rem(zq + o, 4)
        return (y * ZHI + other // 2, lon_of(x, lax.rem(other, 2) * 4 + zr, core))

    def cx_peer(o):
        other = lax.rem(cx + o, NCX)
        return other, (lat, lon_of(other // 2, z_lo, lax.rem(other, 2)))

    far_half = (lat, lon_of(x, lax.rem(z_lo + 4, ZLO), core))
    mine = z_hi * 2 + core

    def sq_peer(o):
        other = lax.rem(mine + o, 4)
        return (y * ZHI + other // 2, lon_of(x, z_lo, lax.rem(other, 2)))

    def midway(lat_, lon_):
        chip_ = lon_ // 2
        x_, z_ = chip_ // ZLO, lax.rem(chip_, ZLO)
        return (lat_, lon_of(x_, lax.rem(z_ + 4, ZLO), lax.rem(lon_, 2)))

    def to_window(ah, bh):
        return midway(lax.rem(lat + nlat - ah, nlat), lax.rem(lon + nlon - bh, nlon))

    def from_window(ah, bh):
        return (lax.rem(lat + ah, nlat), lax.rem(midway(lat, lon)[1] + bh, nlon))

    barrier = pltpu.get_barrier_semaphore()

    def greet(device):
        pl.semaphore_signal(barrier, inc=1, device_id=device, device_id_type=MESH)

    quarters = ((1, 1), (1, 0), (0, 1), (0, 0))
    for ah, bh in quarters:
        greet(from_window(ah, bh))
        greet(to_window(ah, bh))
    greet(core_peer)

    @pl.loop(1, NXY)
    def _(o):
        greet(xy_peer(o)[1])

    for o in range(1, 4):
        greet(zr_peer(o))
        greet(zq_peer(o))
        greet((lat, lon_of(lax.rem(x + o, NX), z_lo, 1 - core)))
    greet((y * ZHI + 1 - z_hi, lon_of(x, z_lo, 1 - core)))

    pairs = (
        (x_hbm, own_x), (g_hbm, own_g), (regions_hbm, regions_ref), (col_hbm, col_ref), (lev_hbm, lev_ref),
        (table_hbm, table_ref), (shift_hbm, shift_ref), (rep_hbm, rep_ref), (heads_hbm, heads_ref),
        (wqkv_hbm, wqkv_ref), (wproj_hbm, wproj_ref), (gain_hbm, gain_ref), (rows_hbm, rows_ref),
        (trows_hbm, trows_ref),
    )
    loads = [pltpu.make_async_copy(src, dst, load_sem.at[n]) for n, (src, dst) in enumerate(pairs)]
    for c in loads:
        c.start()

    for c in loads[:5]:
        c.wait()
    reg_row = jnp.zeros((1, 144), F32)
    for i in range(6):
        reg = regions_ref[i].astype(F32).astype(BF)
        reg_row += jnp.sum(mm(reg, col_ref[...]) * lev_ref[i].astype(F32), axis=0, keepdims=True)
    reg_s[...] = reg_row

    pl.semaphore_wait(barrier, 8 + 1 + (NXY - 1) + 10)

    def remote(src, dst, ss, rs, device):
        return pltpu.make_async_remote_copy(
            src_ref=src, dst_ref=dst, send_sem=ss, recv_sem=rs, device_id=device, device_id_type=MESH
        )

    def here(ah, bh):
        return pl.ds(3 - 3 * ah, 3), pl.ds(6 - 6 * bh, 6)

    def there(ah, bh):
        return pl.ds(3 * ah, 3), pl.ds(6 * bh, 6)

    halo = [remote(reg_s, reg_r, reg_ss, reg_rs, midway(lat, lon))]
    for ah, bh in quarters:
        for n, (src, dst) in enumerate(((own_x, wx), (own_g, wg))):
            at = (ah * 2 + bh) * 2 + n
            halo.append(remote(
                src.at[here(ah, bh)], dst.at[there(ah, bh)], halo_ss.at[at], halo_rs.at[at], to_window(ah, bh)
            ))
    for c in halo:
        c.start()

    for c in loads[5:]:
        c.wait()
    t2[...] = jnp.zeros_like(t2)
    for h in range(6):
        t1[h:h + 1, :] = table_ref[h]
    for l_s in range(2):
        for a_s in range(6):
            la = l_s * 6 + a_s
            for l_t in range(2):
                off = l_s * 1656 + l_t * 828 + a_s * 138
                t2[pl.ds(la * 6, 6), pl.ds(l_t * 138, 138)] = t1[:, pl.ds(off, 138)]
    t_all = t2[...]
    t_hi = t_all.astype(BF)
    t_rest = t_all - t_hi.astype(F32)
    t_mid = t_rest.astype(BF)
    t_lo = (t_rest - t_mid.astype(F32)).astype(BF)

    for b in range(12):
        sel = shift_ref[b]
        bm[pl.ds(b * 72, 72), :] = mmt(t_hi, sel) + mmt(t_mid, sel) + mmt(t_lo, sel)
    rep = rep_ref[...]
    heads = heads_ref[...]
    heads_f = heads.astype(F32)

    halo[0].wait_recv()
    kind = lax.broadcasted_iota(jnp.int32, (8, 144), 0).astype(F32)
    which = (reg_r[...] == kind).astype(F32).astype(BF)
    keep = mm(mmt(rep, which).astype(BF), which)

    for c in halo[1:]:
        c.wait_recv()
    for n in range(72):
        xs[2 * n:2 * n + 2, :] = wx[n // 12, n % 12]
        gs[2 * n:2 * n + 2, :] = wg[n // 12, n % 12]
    win_x = xs[...].astype(F32)
    win_g = gs[...]

    gain = gain_ref[...]
    mean = jnp.mean(win_x, axis=-1, keepdims=True)
    centred = win_x - mean
    inv_std = lax.rsqrt(jnp.mean(centred * centred, axis=-1, keepdims=True) + EPS_NORM)
    standard = centred * inv_std
    normed = (standard * gain).astype(BF)
    projected = mm(normed, wqkv_ref[...])
    q = projected[:, 0:192].astype(BF)
    k = projected[:, 192:384].astype(BF)
    v = projected[:, 384:576].astype(BF)
    grad_mixed = mmt(win_g, wproj_ref[...]).astype(BF)

    qm = (mm(rep, q) * heads_f).astype(BF)
    gm = (mm(rep, grad_mixed) * heads_f).astype(BF)
    scores = jnp.where(keep > 0.5, mmt(qm, k) * SCALE + bm[...], -1e30)
    top = jnp.max(scores, axis=-1, keepdims=True)
    e = jnp.exp(scores - top)
    probs = e / jnp.sum(e, axis=-1, keepdims=True)
    probs_low = probs.astype(BF)
    grad_probs = mmt(gm, v)
    grad_scores = probs * (grad_probs - jnp.sum(probs * grad_probs, axis=-1, keepdims=True))
    gs_low = grad_scores.astype(BF)
    mixed = mtm(rep, (mm(probs_low, v) * heads_f).astype(BF)).astype(BF)
    gq = mtm(rep, (mm(gs_low, k) * SCALE * heads_f).astype(BF))
    gk = mtm(gs_low, qm) * SCALE
    gv = mtm(probs_low, gm)
    gpi = jnp.concatenate([gq, gk, gv], axis=1).astype(BF)

    normed_pad = mm(normed, rows_ref[...]).astype(BF)
    mixed_pad = mm(mixed, rows_ref[...]).astype(BF)
    g_qkv = mtm(normed_pad, gpi)
    g_proj = mtm(mixed_pad, win_g)
    main_f[0] = g_qkv[:, 0:384]
    main_f[1] = jnp.concatenate([g_qkv[:, 384:576], g_proj], axis=1)
    main_s[...] = main_f[1 - core].astype(BF)
    core_rs_copy = remote(main_s, main_r, core_ss, core_rs, core_peer)
    core_rs_copy.start()

    grad_normed = mmt(gpi, wqkv_ref[...])
    gain_raw = jnp.sum(grad_normed * standard, axis=0, keepdims=True)
    t_acc = jnp.zeros((72, 384), F32)
    for b in range(12):
        t_acc += mm(gs_low[b * 72:(b + 1) * 72, :], shift_ref[b])
    tcx_s[...] = mm(trows_ref[...], t_acc.astype(BF)).astype(BF).reshape(8, 16, 384)

    def tcx_copy(o):
        other, device = cx_peer(o)
        return remote(tcx_s.at[other], tcx_r.at[o - 1], tcx_ss.at[o - 1], tcx_rs.at[o - 1], device)

    @pl.loop(1, NCX)
    def _(o):
        tcx_copy(o).start()

    core_rs_copy.wait_recv()
    half = main_f[core] + main_r[...].astype(F32)
    xy_f[...] = half.reshape(16, 16, 384)
    xy_f[0, 12:13, 0:192] = gain_raw
    xy_s[...] = xy_f[...].astype(BF)

    def xy_copy(o):
        other, device = xy_peer(o)
        return remote(xy_s.at[other], xy_r.at[o - 1], xy_ss.at[o - 1], xy_rs.at[o - 1], device)

    @pl.loop(1, NXY)
    def _(o):
        xy_copy(o).start()

    grad_std = grad_normed * gain
    grad_x = inv_std * (
        grad_std
        - jnp.mean(grad_std, axis=-1, keepdims=True)
        - standard * jnp.mean(grad_std * standard, axis=-1, keepdims=True)
    )
    gx[...] = grad_x.astype(BF)
    for n in range(72):
        gxw[n // 12, n % 12] = gx[2 * n:2 * n + 2, :]
    ret_copies = [
        remote(gxw.at[there(ah, bh)], orecv.at[here(ah, bh)], ret_ss.at[ah * 2 + bh], ret_rs.at[ah * 2 + bh], from_window(ah, bh))
        for ah, bh in quarters
    ]
    for c in ret_copies:
        c.start()

    for c in halo + [core_rs_copy]:
        c.wait_send()

    @pl.loop(1, NCX)
    def _(o):
        tcx_copy(o).wait_recv()

    tacc = tcx_s[cx].astype(F32)
    for o in range(NCX - 1):
        tacc += tcx_r[o].astype(F32)
    ta[zr] = tacc.astype(BF)

    def spread(buf, at, ss, rs, peer, n):
        out = [remote(buf.at[at], buf.at[at], ss.at[o - 1], rs.at[o - 1], peer(o)) for o in range(1, n)]
        into = []
        for o in range(1, n):
            slot = buf.at[lax.rem(at + n - o, n)]
            into.append(remote(slot, slot, ss.at[o - 1], rs.at[o - 1], peer(o)))
        return out, into

    ta_out, ta_in = spread(ta, zr, ta_ss, ta_rs, zr_peer, 4)
    for c in ta_out:
        c.start()

    @pl.loop(1, NXY)
    def _(o):
        xy_copy(o).wait_recv()

    acc = xy_f[p]
    for o in range(NXY - 1):
        acc += xy_r[o].astype(F32)
    za[zr] = acc.astype(BF)
    za_out, za_in = spread(za, zr, za_ss, za_rs, zr_peer, 4)
    for c in za_out:
        c.start()

    for c in ta_in:
        c.wait_recv()
    tsum = ta[0].astype(F32)
    for j in range(1, 4):
        tsum += ta[j].astype(F32)
    tb[zhalf] = tsum.astype(BF)
    tb_out, tb_in = spread(tb, zhalf, tb_ss, tb_rs, lambda o: far_half, 2)
    tb_out[0].start()

    for c in za_in:
        c.wait_recv()
    acc = za[0].astype(F32)
    for j in range(1, 4):
        acc += za[j].astype(F32)
    zb[zq] = acc.astype(BF)
    zb_out, zb_in = spread(zb, zq, zb_ss, zb_rs, zq_peer, 4)
    for c in zb_out:
        c.start()

    tb_in[0].wait_recv()
    tpiece = tb[0].astype(F32) + tb[1].astype(F32)
    tpiece_low = tpiece.astype(BF)
    tpiece = tpiece_low.astype(F32)
    squares = jnp.sum(jnp.sum(tpiece * tpiece, axis=1, keepdims=True), axis=0, keepdims=True)
    sq[mine] = jnp.broadcast_to(squares, (1, 128))
    sq_out, sq_in = spread(sq, mine, sq_ss, sq_rs, sq_peer, 4)
    for c in sq_out:
        c.start()
    tfin[cx] = tpiece_low

    def tcag_copy(o):
        _, device = cx_peer(o)
        return remote(tfin.at[cx], tfin.at[cx], tcag_ss.at[o - 1], tcag_rs.at[o - 1], device)

    @pl.loop(1, NCX)
    def _(o):
        tcag_copy(o).start()

    for c in ret_copies:
        c.wait()
    out_x[...] = (own_g[...].astype(F32) + orecv[...].astype(F32)).astype(BF)

    @pl.loop(1, NXY)
    def _(o):
        xy_copy(o).wait_send()

    @pl.loop(1, NCX)
    def _(o):
        tcx_copy(o).wait_send()

    for c in ta_out + za_out + tb_out:
        c.wait_send()

    for c in zb_in:
        c.wait_recv()
    acc = zb[0].astype(F32)
    for j in range(1, 4):
        acc += zb[j].astype(F32)
    piece[...] = acc
    for c in sq_in:
        c.wait_recv()
    both = (sq[0] + sq[1]) + (sq[2] + sq[3])
    both_hi = both.astype(BF).astype(F32)
    both_mid = (both - both_hi).astype(BF).astype(F32)
    both_lo = both - both_hi - both_mid
    lane = lax.broadcasted_iota(jnp.int32, (1, 128), 1)
    piece[13:14, 0:128] = jnp.where(
        lane == 0, both_hi, jnp.where(lane == 1, both_mid, jnp.where(lane == 2, both_lo, 0.0))
    )
    fin[core, p] = piece[...].astype(BF)

    def xyag_copy(o):
        _, device = xy_peer(o)
        return remote(fin.at[core, p], fin.at[core, p], xyag_ss.at[o - 1], xyag_rs.at[o - 1], device)

    @pl.loop(1, NXY)
    def _(o):
        xyag_copy(o).start()

    @pl.loop(1, NCX)
    def _(o):
        other = lax.rem(cx + NCX - o, NCX)
        slot = tfin.at[other]
        remote(slot, slot, tcag_ss.at[o - 1], tcag_rs.at[o - 1], cx_peer(o)[1]).wait_recv()

    band = mtm(trows_ref[...], tfin[...].reshape(128, 384))

    @pl.loop(1, NCX)
    def _(o):
        tcag_copy(o).wait_send()

    for c in zb_out + sq_out:
        c.wait_send()

    @pl.loop(1, NXY)
    def _(o):
        other = lax.rem(p + NXY - o, NXY)
        slot = fin.at[core, other]
        remote(slot, slot, xyag_ss.at[o - 1], xyag_rs.at[o - 1], xy_peer(o)[1]).wait_recv()

    cag = remote(fin.at[core], fin.at[core], cag_ss, cag_rs, core_peer)
    cag.start()

    @pl.loop(1, NXY)
    def _(o):
        xyag_copy(o).wait_send()

    shares = jnp.zeros((1, 128), F32)
    for j in range(NXY):
        shares += fin[core, j, 13:14, 0:128].astype(F32)
    total = jnp.sum(shares, axis=1, keepdims=True)
    band = band * (1.0 / jnp.sqrt(total / (NLAT * 6 * 3312) + EPS_RMS))
    for l_s in range(2):
        for a_s in range(6):
            la = l_s * 6 + a_s
            for l_t in range(2):
                off = l_s * 1656 + l_t * 828 + a_s * 138
                t1[:, pl.ds(off, 138)] = band[la * 6:la * 6 + 6, l_t * 138:l_t * 138 + 138]
    for h in range(6):
        out_table[h] = t1[h:h + 1, :]

    def squares_of(value):
        return jnp.sum(jnp.sum(value * value, axis=1, keepdims=True), axis=0, keepdims=True)

    def part(which_core):
        value = mm(rows_ref[...], fin[which_core].reshape(256, 384))
        return value, squares_of(value[:, 0:192]), squares_of(value[:, 192:384]), fin[which_core, 0, 12:13, 0:192].astype(F32)

    own = part(core)
    other_half = fin.at[1 - core]
    remote(other_half, other_half, cag_ss, cag_rs, core_peer).wait_recv()
    theirs = part(1 - core)
    first = [jnp.where(core == 0, a, b) for a, b in zip(own, theirs)]
    second = [jnp.where(core == 0, b, a) for a, b in zip(own, theirs)]

    def scale_of(total, entries):
        return 1.0 / jnp.sqrt(total / entries + EPS_RMS)

    s_qkv = scale_of(first[1] + first[2] + second[1], 192 * 576)
    s_proj = scale_of(second[2], 192 * 192)
    out_qkv[:, 0:384] = first[0] * s_qkv
    out_qkv[:, 384:576] = second[0][:, 0:192] * s_qkv
    out_proj[...] = second[0][:, 192:384] * s_proj
    w_g = first[3] + second[3]
    out_gain[...] = w_g * scale_of(squares_of(w_g), 192)
    cag.wait_send()


def hand_over(*refs):
    sem = refs[-1]
    n = (len(refs) - 1) // 2
    copies = [pltpu.make_async_copy(refs[i], refs[n + i], sem.at[i]) for i in range(n)]
    for c in copies:
        c.start()
    for c in copies:
        c.wait()


def on_device(activations, cotangent, gain, w_qkv, w_proj, bias_table, regions):
    consts = [jnp.asarray(m) for m in tables()]
    vmem = pl.BlockSpec(memory_space=pltpu.VMEM)
    hbm = pl.BlockSpec(memory_space=pltpu.HBM)
    dma = pltpu.SemaphoreType.DMA
    operands = [
        activations.transpose(1, 2, 0, 3), cotangent.transpose(1, 2, 0, 3), gain.reshape(1, 192), w_qkv, w_proj,
        bias_table.transpose(1, 0, 2), regions.transpose(1, 0, 2), *consts,
    ]
    scratch = [pltpu.VMEM(o.shape, o.dtype) for o in operands[2:]] + [
        pltpu.VMEM((6, 12, 2, 192), BF), pltpu.VMEM((6, 12, 2, 192), BF), pltpu.VMEM((1, 144), F32), pltpu.VMEM((1, 144), F32),
        pltpu.VMEM((6, 12, 2, 192), BF), pltpu.VMEM((6, 12, 2, 192), BF), pltpu.VMEM((6, 12, 2, 192), BF), pltpu.VMEM((6, 12, 2, 192), BF),
        pltpu.VMEM((144, 192), BF), pltpu.VMEM((144, 192), BF), pltpu.VMEM((144, 192), BF),
        pltpu.VMEM((6, 3312), F32), pltpu.VMEM((72, 384), F32), pltpu.VMEM((864, 144), F32),
        pltpu.VMEM((2, 256, 384), F32), pltpu.VMEM((256, 384), BF), pltpu.VMEM((256, 384), BF),
        pltpu.VMEM((16, 16, 384), F32), pltpu.VMEM((16, 16, 384), BF), pltpu.VMEM((15, 16, 384), BF),
        pltpu.VMEM((4, 16, 384), BF), pltpu.VMEM((4, 16, 384), BF), pltpu.VMEM((16, 384), F32),
        pltpu.VMEM((2, 16, 16, 384), BF),
        pltpu.VMEM((8, 16, 384), BF), pltpu.VMEM((7, 16, 384), BF),
        pltpu.VMEM((4, 16, 384), BF), pltpu.VMEM((2, 16, 384), BF),
        pltpu.VMEM((8, 16, 384), BF), pltpu.VMEM((4, 1, 128), F32),
        dma((14,)), dma, dma, dma((8,)), dma((8,)), dma((4,)), dma((4,)), dma, dma,
        dma((15,)), dma((15,)), dma((3,)), dma((3,)), dma((3,)), dma((3,)),
        dma((15,)), dma((15,)), dma, dma,
        dma((7,)), dma((7,)), dma((3,)), dma((3,)), dma((1,)), dma((1,)), dma((7,)), dma((7,)), dma((3,)), dma((3,)),
    ]
    shapes = (
        jax.ShapeDtypeStruct((6, 12, 2, 192), BF),
        jax.ShapeDtypeStruct((192, 576), F32),
        jax.ShapeDtypeStruct((192, 192), F32),
        jax.ShapeDtypeStruct((1, 192), F32),
        jax.ShapeDtypeStruct((6, 1, 3312), F32),
    )
    outs = pl.pallas_call(
        kernel,
        out_shape=shapes,
        in_specs=[hbm] * len(operands),
        out_specs=(vmem,) * 5,
        scratch_shapes=scratch,
        compiler_params=pltpu.CompilerParams(
            collective_id=0, has_side_effects=True, vmem_limit_bytes=40 * 1024 * 1024
        ),
        name="swin_backward",
    )(*[pltpu.with_memory_space_constraint(o, pltpu.HBM) for o in operands])
    outs = pl.pallas_call(
        hand_over,
        out_shape=shapes,
        in_specs=[vmem] * 5,
        out_specs=(hbm,) * 5,
        scratch_shapes=[dma((5,))],
        compiler_params=pltpu.CompilerParams(vmem_limit_bytes=32 * 1024 * 1024),
        name="hand_over",
    )(*outs)
    return outs[0].transpose(2, 0, 1, 3), outs[1], outs[2], outs[3].reshape(192), outs[4].transpose(1, 0, 2)


def solution(mesh):
    in_specs = (
        P(None, "lat", "lon", None),
        P(None, "lat", "lon", None),
        P(),
        P(),
        P(),
        P("lat", None, None),
        P(None, "lat", "lon"),
    )
    out_specs = (P(None, "lat", "lon", None), P(), P(), P(), P("lat", None, None))
    return jax.shard_map(
        on_device, mesh=mesh, in_specs=in_specs, out_specs=out_specs, check_vma=False
    )
```

```python
import functools

import jax
import jax.numpy as jnp
import ml_dtypes
import numpy as np
from jax import lax
from jax.experimental import pallas as pl
from jax.experimental.pallas import tpu as pltpu
from jax.sharding import PartitionSpec as P

F32 = jnp.float32
BF = jnp.bfloat16
MESH = pl.DeviceIdType.MESH

EPS_NORM = 1e-05
EPS_RMS = 1e-06
SCALE = 32.0 ** -0.5

NX, NY, ZHI, ZLO = 4, 4, 2, 8
NXY = NX * NY
NLAT = NY * ZHI
NCX = NX * 2
OWNERS = [(i, j) for i in range(NX) for j in range(NY) if i != j] + [(0, 0)]
PIECES = len(OWNERS)


def tables():
    tok = np.arange(144)
    ta, tb, tl = tok // 24, tok // 2 % 12, 1 - tok % 2
    la = tl * 6 + ta
    row = np.arange(864)
    rb, rla, rh = row // 72, row // 6 % 12, row % 6
    rep = (rb[:, None] == tb[None, :]) & (rla[:, None] == la[None, :])
    heads = rh[:, None] == np.arange(192)[None, :] // 32
    shift = np.zeros((12, 144, 384), np.float32)
    for bs in range(12):
        shift[bs, tok, la * 23 + tb - bs + 11] = 1
    trows = np.zeros((128, 72), np.float32)
    r = np.arange(72)
    trows[r // 9 * 16 + r % 9, r] = 1
    col = tb[None, :] == np.arange(12)[:, None]
    lev = (ta[None, None, :] == np.arange(6)[:, None, None]) & (tl[None, None, :] == np.arange(2)[None, :, None])
    return [
        np.ascontiguousarray(m).astype(ml_dtypes.bfloat16)
        for m in (rep, heads, shift, trows, col, lev)
    ]


def mm(a, b):
    return lax.dot_general(a, b, (((1,), (0,)), ((), ())), preferred_element_type=F32)


def mmt(a, b):
    return lax.dot_general(a, b, (((1,), (1,)), ((), ())), preferred_element_type=F32)


def mtm(a, b):
    return lax.dot_general(a, b, (((0,), (0,)), ((), ())), preferred_element_type=F32)


def kernel(
    x_hbm, g_hbm, gain_hbm, wqkv_hbm, wproj_hbm, table_hbm, regions_hbm,
    rep_hbm, heads_hbm, shift_hbm, trows_hbm, col_hbm, lev_hbm,
    out_x, out_qkv, out_proj, out_gain, out_table,
    gain_ref, wqkv_ref, wproj_ref, table_ref, regions_ref,
    rep_ref, heads_ref, shift_ref, trows_ref, col_ref, lev_ref,
    own_x, own_g, reg_s, reg_r, pack, win, gxw, orecv, xg, gx, t1, t2, bm,
    main_f, main_s, main_r, xy_f, xy_s, xy_r, za, zb, fin,
    tcx_s, tcx_r, ta, tb, tfin, sq,
    load_sem, reg_ss, reg_rs, halo_ss, halo_rs, ret_ss, ret_rs, core_ss, core_rs, xy_ss, xy_rs, za_ss, za_rs, zb_ss, zb_rs,
    xyag_ss, xyag_rs, cag_ss, cag_rs,
    tcx_ss, tcx_rs, ta_ss, ta_rs, tb_ss, tb_rs, tcag_ss, tcag_rs, sq_ss, sq_rs,
):
    lat = lax.axis_index("lat")
    lon = lax.axis_index("lon")
    nlat, nlon = NLAT, NX * ZLO * 2
    y, z_hi = lat // ZHI, lax.rem(lat, ZHI)
    core = lax.rem(lon, 2)
    chip = lon // 2
    x, z_lo = chip // ZLO, lax.rem(chip, ZLO)
    zq, zr = z_hi * 2 + z_lo // 4, lax.rem(z_lo, 4)
    zhalf = z_lo // 4
    p = x * NY + y
    cx = x * 2 + core

    def lon_of(x_, z_lo_, core_):
        return (x_ * ZLO + z_lo_) * 2 + core_

    core_peer = (lat, lon_of(x, z_lo, 1 - core))

    def xy_peer(o):
        other = lax.rem(p + o, NXY)
        return other, ((other // NY) * 0 + lax.rem(other, NY) * ZHI + z_hi, lon_of(other // NY, z_lo, core))

    def zr_peer(o):
        return (lat, lon_of(x, zhalf * 4 + lax.rem(zr + o, 4), core))

    def zq_peer(o):
        other = lax.rem(zq + o, 4)
        return (y * ZHI + other // 2, lon_of(x, lax.rem(other, 2) * 4 + zr, core))

    def cx_peer(o):
        other = lax.rem(cx + o, NCX)
        return other, (lat, lon_of(other // 2, z_lo, lax.rem(other, 2)))

    far_half = (lat, lon_of(x, lax.rem(z_lo + 4, ZLO), core))
    owner = jnp.logical_or(x != y, x == 0)
    w = jnp.where(x == y, PIECES - 1, x * (NY - 1) + y - (y > x).astype(jnp.int32))

    def place(n):
        i, j = OWNERS[n]
        return i * NY + j, (j * ZHI + z_hi, lon_of(i, z_lo, core))

    def lat_peer(o):
        return (lax.rem(lat + o, NLAT), lon)

    def midway(lat_, lon_):
        chip_ = lon_ // 2
        x_, z_ = chip_ // ZLO, lax.rem(chip_, ZLO)
        return (lat_, lon_of(x_, lax.rem(z_ + 4, ZLO), lax.rem(lon_, 2)))

    def to_window(ah, bh):
        return midway(lax.rem(lat + nlat - ah, nlat), lax.rem(lon + nlon - bh, nlon))

    def from_window(ah, bh):
        return (lax.rem(lat + ah, nlat), lax.rem(midway(lat, lon)[1] + bh, nlon))

    barrier = pltpu.get_barrier_semaphore()

    def greet(device):
        pl.semaphore_signal(barrier, inc=1, device_id=device, device_id_type=MESH)

    quarters = ((1, 1), (1, 0), (0, 1), (0, 0))
    for ah, bh in quarters:
        greet(from_window(ah, bh))
        greet(to_window(ah, bh))
    greet(core_peer)

    @pl.loop(1, NXY)
    def _(o):
        greet(xy_peer(o)[1])

    for o in range(1, 4):
        greet(zr_peer(o))
        greet(zq_peer(o))
        greet((lat, lon_of(lax.rem(x + o, NX), z_lo, 1 - core)))
        greet((lax.rem(y + o, NY) * ZHI + 1 - z_hi, lon))

    pairs = (
        (x_hbm, own_x), (g_hbm, own_g), (regions_hbm, regions_ref), (col_hbm, col_ref), (lev_hbm, lev_ref),
        (table_hbm, table_ref), (shift_hbm, shift_ref), (rep_hbm, rep_ref), (heads_hbm, heads_ref),
        (wqkv_hbm, wqkv_ref), (wproj_hbm, wproj_ref), (gain_hbm, gain_ref),
        (trows_hbm, trows_ref),
    )
    loads = [pltpu.make_async_copy(src, dst, load_sem.at[n]) for n, (src, dst) in enumerate(pairs)]
    for c in loads:
        c.start()

    for c in loads[:5]:
        c.wait()
    reg_row = jnp.zeros((1, 144), F32)
    for i in range(6):
        reg = regions_ref[i].astype(F32).astype(BF)
        reg_row += jnp.sum(mm(reg, col_ref[...]) * lev_ref[i].astype(F32), axis=0, keepdims=True)
    reg_s[...] = reg_row

    pack[:, :, 0] = own_x[:, :, :, 0:128]
    pack[:, :, 1] = own_g[:, :, :, 0:128]
    pack[:, :, 2] = jnp.concatenate([own_x[:, :, :, 128:192], own_g[:, :, :, 128:192]], axis=-1)

    pl.semaphore_wait(barrier, 8 + 1 + (NXY - 1) + 12)

    def remote(src, dst, ss, rs, device):
        return pltpu.make_async_remote_copy(
            src_ref=src, dst_ref=dst, send_sem=ss, recv_sem=rs, device_id=device, device_id_type=MESH
        )

    def here(ah, bh):
        return pl.ds(3 - 3 * ah, 3), pl.ds(6 - 6 * bh, 6)

    def there(ah, bh):
        return pl.ds(3 * ah, 3), pl.ds(6 * bh, 6)

    halo = [remote(reg_s, reg_r, reg_ss, reg_rs, midway(lat, lon))]
    for ah, bh in quarters:
        at = ah * 2 + bh
        halo.append(remote(
            pack.at[here(ah, bh)], win.at[there(ah, bh)], halo_ss.at[at], halo_rs.at[at], to_window(ah, bh)
        ))
    for c in halo:
        c.start()

    for c in loads[5:]:
        c.wait()
    t2[...] = jnp.zeros_like(t2)
    for h in range(6):
        t1[h:h + 1, :] = table_ref[h]
    for l_s in range(2):
        for a_s in range(6):
            la = l_s * 6 + a_s
            for l_t in range(2):
                off = l_s * 1656 + l_t * 828 + a_s * 138
                t2[pl.ds(la * 6, 6), pl.ds(l_t * 138, 138)] = t1[:, pl.ds(off, 138)]
    t_all = t2[...]
    t_hi = t_all.astype(BF)
    t_rest = t_all - t_hi.astype(F32)
    t_mid = t_rest.astype(BF)
    t_lo = (t_rest - t_mid.astype(F32)).astype(BF)

    for b in range(12):
        sel = shift_ref[b]
        bm[pl.ds(b * 72, 72), :] = mmt(t_hi, sel) + mmt(t_mid, sel) + mmt(t_lo, sel)
    rep = rep_ref[...]
    heads = heads_ref[...]
    heads_f = heads.astype(F32)

    halo[0].wait_recv()
    kind = lax.broadcasted_iota(jnp.int32, (8, 144), 0).astype(F32)
    which = (reg_r[...] == kind).astype(F32).astype(BF)
    keep = mm(mmt(rep, which).astype(BF), which)

    for c in halo[1:]:
        c.wait_recv()
    for n in range(72):
        for c in range(3):
            xg[2 * n:2 * n + 2, c * 128:c * 128 + 128] = win[n // 12, n % 12, c]
    high = xg[:, 256:384].astype(F32)
    win_x = jnp.concatenate([xg[:, 0:128].astype(F32), high[:, 0:64]], axis=1)
    win_g = jnp.concatenate([xg[:, 128:256].astype(F32), high[:, 64:128]], axis=1).astype(BF)

    gain = gain_ref[...]
    mean = jnp.mean(win_x, axis=-1, keepdims=True)
    centred = win_x - mean
    inv_std = lax.rsqrt(jnp.mean(centred * centred, axis=-1, keepdims=True) + EPS_NORM)
    standard = centred * inv_std
    normed = (standard * gain).astype(BF)
    projected = mm(normed, wqkv_ref[...])
    q = projected[:, 0:192].astype(BF)
    k = projected[:, 192:384].astype(BF)
    v = projected[:, 384:576].astype(BF)
    grad_mixed = mmt(win_g, wproj_ref[...]).astype(BF)

    qm = (mm(rep, q) * heads_f).astype(BF)
    gm = (mm(rep, grad_mixed) * heads_f).astype(BF)
    scores = jnp.where(keep > 0.5, mmt(qm, k) * SCALE + bm[...], -1e30)
    top = jnp.max(scores, axis=-1, keepdims=True)
    e = jnp.exp(scores - top)
    probs = e / jnp.sum(e, axis=-1, keepdims=True)
    probs_low = probs.astype(BF)
    grad_probs = mmt(gm, v)
    grad_scores = probs * (grad_probs - jnp.sum(probs * grad_probs, axis=-1, keepdims=True))
    gs_low = grad_scores.astype(BF)
    mixed = mtm(rep, (mm(probs_low, v) * heads_f).astype(BF)).astype(BF)
    gq = mtm(rep, (mm(gs_low, k) * SCALE * heads_f).astype(BF))
    gk = mtm(gs_low, qm) * SCALE
    gv = mtm(probs_low, gm)
    gpi = jnp.concatenate([gq, gk, gv], axis=1).astype(BF)

    g_qkv = mtm(normed, gpi)
    main_f[0] = g_qkv[:, 0:384]
    main_f[1] = jnp.concatenate([g_qkv[:, 384:576], mtm(mixed, win_g)], axis=1)
    main_s[...] = main_f[1 - core].astype(BF)
    core_rs_copy = remote(main_s, main_r, core_ss, core_rs, core_peer)
    core_rs_copy.start()

    grad_normed = mmt(gpi, wqkv_ref[...])
    gain_raw = jnp.sum(grad_normed * standard, axis=0, keepdims=True)
    t_acc = jnp.zeros((72, 384), F32)
    for b in range(12):
        t_acc += mm(gs_low[b * 72:(b + 1) * 72, :], shift_ref[b])
    tcx_s[...] = mm(trows_ref[...], t_acc.astype(BF)).astype(BF).reshape(8, 16, 384)

    def tcx_copy(o):
        other, device = cx_peer(o)
        return remote(tcx_s.at[other], tcx_r.at[o - 1], tcx_ss.at[o - 1], tcx_rs.at[o - 1], device)

    @pl.loop(1, NCX)
    def _(o):
        tcx_copy(o).start()

    core_rs_copy.wait_recv()
    both_cores = main_f[core] + main_r[...].astype(F32)
    xy_f[0:PIECES - 1] = both_cores.reshape(PIECES - 1, 16, 384)
    xy_f[PIECES - 1] = jnp.zeros((16, 384), F32)
    xy_f[PIECES - 1, 0:1, 0:192] = gain_raw
    xy_s[...] = xy_f[...].astype(BF)
    xy_r[p] = jnp.zeros((16, 384), BF)

    def xy_copy(n):
        at, device = place(n)
        return at, remote(xy_s.at[n], xy_r.at[p], xy_ss.at[n], xy_rs.at[p], device)

    for n in range(PIECES):
        at, c = xy_copy(n)

        @pl.when(p != at)
        def _(c=c):
            c.start()

    grad_std = grad_normed * gain
    grad_x = inv_std * (
        grad_std
        - jnp.mean(grad_std, axis=-1, keepdims=True)
        - standard * jnp.mean(grad_std * standard, axis=-1, keepdims=True)
    )
    gx[...] = grad_x.astype(BF)
    for n in range(72):
        gxw[n // 12, n % 12] = gx[2 * n:2 * n + 2, :]
    ret_copies = [
        remote(gxw.at[there(ah, bh)], orecv.at[here(ah, bh)], ret_ss.at[ah * 2 + bh], ret_rs.at[ah * 2 + bh], from_window(ah, bh))
        for ah, bh in quarters
    ]

    for c in halo + [core_rs_copy]:
        c.wait_send()

    @pl.loop(1, NCX)
    def _(o):
        tcx_copy(o).wait_recv()

    tacc = tcx_s[cx].astype(F32)
    for o in range(NCX - 1):
        tacc += tcx_r[o].astype(F32)
    ta[zr] = tacc.astype(BF)

    def spread(buf, at, ss, rs, peer, n):
        out = [remote(buf.at[at], buf.at[at], ss.at[o - 1], rs.at[o - 1], peer(o)) for o in range(1, n)]
        into = []
        for o in range(1, n):
            slot = buf.at[lax.rem(at + n - o, n)]
            into.append(remote(slot, slot, ss.at[o - 1], rs.at[o - 1], peer(o)))
        return out, into

    ta_out, ta_in = spread(ta, zr, ta_ss, ta_rs, zr_peer, 4)
    for c in ta_out:
        c.start()

    za_out, za_in = spread(za, zr, za_ss, za_rs, zr_peer, 4)

    @pl.when(owner)
    def _():
        for j in range(NXY):
            @pl.when(p != j)
            def _(j=j):
                remote(xy_s.at[0], xy_r.at[j], xy_ss.at[0], xy_rs.at[j], core_peer).wait_recv()

        acc = xy_f[w]
        for j in range(NXY):
            acc += xy_r[j].astype(F32)
        za[zr] = acc.astype(BF)
        for c in za_out:
            c.start()

    for c in ta_in:
        c.wait_recv()
    tsum = ta[0].astype(F32)
    for j in range(1, 4):
        tsum += ta[j].astype(F32)
    tb[zhalf] = tsum.astype(BF)
    tb_out, tb_in = spread(tb, zhalf, tb_ss, tb_rs, lambda o: far_half, 2)
    tb_out[0].start()

    zb_out, zb_in = spread(zb, zq, zb_ss, zb_rs, zq_peer, 4)

    @pl.when(owner)
    def _():
        for c in za_in:
            c.wait_recv()
        acc = za[0].astype(F32)
        for j in range(1, 4):
            acc += za[j].astype(F32)
        zb[zq] = acc.astype(BF)
        for c in zb_out:
            c.start()

    for c in ret_copies:
        c.start()

    tb_in[0].wait_recv()
    tfin[cx] = (tb[0].astype(F32) + tb[1].astype(F32)).astype(BF)

    def tcag_copy(o):
        _, device = cx_peer(o)
        return remote(tfin.at[cx], tfin.at[cx], tcag_ss.at[o - 1], tcag_rs.at[o - 1], device)

    @pl.loop(1, NCX)
    def _(o):
        tcag_copy(o).start()

    for n in range(PIECES):
        at, c = xy_copy(n)

        @pl.when(p != at)
        def _(c=c):
            c.wait_send()

    @pl.loop(1, NCX)
    def _(o):
        tcx_copy(o).wait_send()

    for c in ta_out + tb_out:
        c.wait_send()

    @pl.loop(1, NCX)
    def _(o):
        other = lax.rem(cx + NCX - o, NCX)
        slot = tfin.at[other]
        remote(slot, slot, tcag_ss.at[o - 1], tcag_rs.at[o - 1], cx_peer(o)[1]).wait_recv()

    def squares_of(value):
        return jnp.sum(jnp.sum(value * value, axis=1, keepdims=True), axis=0, keepdims=True)

    band = mtm(trows_ref[...], tfin[...].reshape(128, 384))
    sq[lat] = jnp.broadcast_to(squares_of(band), (1, 128))
    sq_out, sq_in = spread(sq, lat, sq_ss, sq_rs, lat_peer, NLAT)
    for c in sq_out:
        c.start()

    def xyag_copy(o):
        _, device = xy_peer(o)
        return remote(fin.at[core, w], fin.at[core, w], xyag_ss.at[o - 1], xyag_rs.at[w], device)

    @pl.when(owner)
    def _():
        for c in za_out:
            c.wait_send()
        for c in zb_in:
            c.wait_recv()
        acc = zb[0].astype(F32)
        for j in range(1, 4):
            acc += zb[j].astype(F32)
        fin[core, w] = acc.astype(BF)

        @pl.loop(1, NXY)
        def _(o):
            xyag_copy(o).start()

    for c in ret_copies:
        c.wait()
    out_x[...] = (own_g[...].astype(F32) + orecv[...].astype(F32)).astype(BF)

    @pl.loop(1, NCX)
    def _(o):
        tcag_copy(o).wait_send()

    @pl.when(owner)
    def _():
        for c in zb_out:
            c.wait_send()

    for n in range(PIECES):
        at, device = place(n)

        @pl.when(p != at)
        def _(n=n, device=device):
            slot = fin.at[core, n]
            remote(slot, slot, xyag_ss.at[0], xyag_rs.at[n], device).wait_recv()

    cag = remote(fin.at[core], fin.at[core], cag_ss, cag_rs, core_peer)
    cag.start()

    @pl.when(owner)
    def _():
        @pl.loop(1, NXY)
        def _(o):
            xyag_copy(o).wait_send()

    for c in sq_in:
        c.wait_recv()
    total = sq[0]
    for j in range(1, NLAT):
        total += sq[j]
    total = total[:, 0:1]
    band = band * (1.0 / jnp.sqrt(total / (NLAT * 6 * 3312) + EPS_RMS))
    for l_s in range(2):
        for a_s in range(6):
            la = l_s * 6 + a_s
            for l_t in range(2):
                off = l_s * 1656 + l_t * 828 + a_s * 138
                t1[:, pl.ds(off, 138)] = band[la * 6:la * 6 + 6, l_t * 138:l_t * 138 + 138]
    for h in range(6):
        out_table[h] = t1[h:h + 1, :]
    for c in sq_out:
        c.wait_send()

    def part(which_core):
        value = fin[which_core, 0:PIECES - 1].reshape(192, 384).astype(F32)
        return value, squares_of(value[:, 0:192]), squares_of(value[:, 192:384]), fin[which_core, PIECES - 1, 0:1, 0:192].astype(F32)

    own = part(core)
    other_half = fin.at[1 - core]
    remote(other_half, other_half, cag_ss, cag_rs, core_peer).wait_recv()
    theirs = part(1 - core)
    first = [jnp.where(core == 0, a, b) for a, b in zip(own, theirs)]
    second = [jnp.where(core == 0, b, a) for a, b in zip(own, theirs)]

    def scale_of(total, entries):
        return 1.0 / jnp.sqrt(total / entries + EPS_RMS)

    s_qkv = scale_of(first[1] + first[2] + second[1], 192 * 576)
    s_proj = scale_of(second[2], 192 * 192)
    out_qkv[:, 0:384] = first[0] * s_qkv
    out_qkv[:, 384:576] = second[0][:, 0:192] * s_qkv
    out_proj[...] = second[0][:, 192:384] * s_proj
    w_g = first[3] + second[3]
    out_gain[...] = w_g * scale_of(squares_of(w_g), 192)
    cag.wait_send()


def hand_over(*refs):
    sem = refs[-1]
    n = (len(refs) - 1) // 2
    copies = [pltpu.make_async_copy(refs[i], refs[n + i], sem.at[i]) for i in range(n)]
    for c in copies:
        c.start()
    for c in copies:
        c.wait()


def on_device(activations, cotangent, gain, w_qkv, w_proj, bias_table, regions):
    consts = [jnp.asarray(m) for m in tables()]
    vmem = pl.BlockSpec(memory_space=pltpu.VMEM)
    hbm = pl.BlockSpec(memory_space=pltpu.HBM)
    dma = pltpu.SemaphoreType.DMA
    operands = [
        activations.transpose(1, 2, 0, 3), cotangent.transpose(1, 2, 0, 3), gain.reshape(1, 192), w_qkv, w_proj,
        bias_table.transpose(1, 0, 2), regions.transpose(1, 0, 2), *consts,
    ]
    scratch = [pltpu.VMEM(o.shape, o.dtype) for o in operands[2:]] + [
        pltpu.VMEM((6, 12, 2, 192), BF), pltpu.VMEM((6, 12, 2, 192), BF), pltpu.VMEM((1, 144), F32), pltpu.VMEM((1, 144), F32),
        pltpu.VMEM((6, 12, 3, 2, 128), BF), pltpu.VMEM((6, 12, 3, 2, 128), BF),
        pltpu.VMEM((6, 12, 2, 192), BF), pltpu.VMEM((6, 12, 2, 192), BF),
        pltpu.VMEM((144, 384), BF), pltpu.VMEM((144, 192), BF),
        pltpu.VMEM((6, 3312), F32), pltpu.VMEM((72, 384), F32), pltpu.VMEM((864, 144), F32),
        pltpu.VMEM((2, 192, 384), F32), pltpu.VMEM((192, 384), BF), pltpu.VMEM((192, 384), BF),
        pltpu.VMEM((PIECES, 16, 384), F32), pltpu.VMEM((PIECES, 16, 384), BF), pltpu.VMEM((16, 16, 384), BF),
        pltpu.VMEM((4, 16, 384), BF), pltpu.VMEM((4, 16, 384), BF), pltpu.VMEM((2, PIECES, 16, 384), BF),
        pltpu.VMEM((8, 16, 384), BF), pltpu.VMEM((7, 16, 384), BF),
        pltpu.VMEM((4, 16, 384), BF), pltpu.VMEM((2, 16, 384), BF),
        pltpu.VMEM((8, 16, 384), BF), pltpu.VMEM((NLAT, 1, 128), F32),
        dma((13,)), dma, dma, dma((4,)), dma((4,)), dma((4,)), dma((4,)), dma, dma,
        dma((PIECES,)), dma((16,)), dma((3,)), dma((3,)), dma((3,)), dma((3,)),
        dma((15,)), dma((PIECES,)), dma, dma,
        dma((7,)), dma((7,)), dma((3,)), dma((3,)), dma((1,)), dma((1,)), dma((7,)), dma((7,)), dma((7,)), dma((7,)),
    ]
    shapes = (
        jax.ShapeDtypeStruct((6, 12, 2, 192), BF),
        jax.ShapeDtypeStruct((192, 576), F32),
        jax.ShapeDtypeStruct((192, 192), F32),
        jax.ShapeDtypeStruct((1, 192), F32),
        jax.ShapeDtypeStruct((6, 1, 3312), F32),
    )
    outs = pl.pallas_call(
        kernel,
        out_shape=shapes,
        in_specs=[hbm] * len(operands),
        out_specs=(vmem,) * 5,
        scratch_shapes=scratch,
        compiler_params=pltpu.CompilerParams(
            collective_id=0, has_side_effects=True, vmem_limit_bytes=40 * 1024 * 1024
        ),
        name="swin_backward",
    )(*[pltpu.with_memory_space_constraint(o, pltpu.HBM) for o in operands])
    outs = pl.pallas_call(
        hand_over,
        out_shape=shapes,
        in_specs=[vmem] * 5,
        out_specs=(hbm,) * 5,
        scratch_shapes=[dma((5,))],
        compiler_params=pltpu.CompilerParams(vmem_limit_bytes=32 * 1024 * 1024),
        name="hand_over",
    )(*outs)
    return outs[0].transpose(2, 0, 1, 3), outs[1], outs[2], outs[3].reshape(192), outs[4].transpose(1, 0, 2)


def solution(mesh):
    in_specs = (
        P(None, "lat", "lon", None),
        P(None, "lat", "lon", None),
        P(),
        P(),
        P(),
        P("lat", None, None),
        P(None, "lat", "lon"),
    )
    out_specs = (P(None, "lat", "lon", None), P(), P(), P(), P("lat", None, None))
    return jax.shard_map(
        on_device, mesh=mesh, in_specs=in_specs, out_specs=out_specs, check_vma=False
    )
```

```python
import functools

import jax
import jax.numpy as jnp
import ml_dtypes
import numpy as np
from jax import lax
from jax.experimental import pallas as pl
from jax.experimental.pallas import tpu as pltpu
from jax.sharding import PartitionSpec as P

F32 = jnp.float32
BF = jnp.bfloat16
MESH = pl.DeviceIdType.MESH

EPS_NORM = 1e-05
EPS_RMS = 1e-06
SCALE = 32.0 ** -0.5

NX, NY, ZHI, ZLO = 4, 4, 2, 8
NXY = NX * NY
NLAT = NY * ZHI
NCX = NX * 2
OWNERS = [(i, j) for i in range(NX) for j in range(NY) if i != j] + [(0, 0)]
PIECES = len(OWNERS)


def tables():
    tok = np.arange(144)
    ta, tb, tl = tok // 24, tok // 2 % 12, 1 - tok % 2
    la = tl * 6 + ta
    row = np.arange(864)
    rb, rla, rh = row // 72, row // 6 % 12, row % 6
    rep = (rb[:, None] == tb[None, :]) & (rla[:, None] == la[None, :])
    heads = rh[:, None] == np.arange(192)[None, :] // 32
    shift = np.zeros((12, 144, 384), np.float32)
    for bs in range(12):
        shift[bs, tok, la * 23 + tb - bs + 11] = 1
    trows = np.zeros((128, 72), np.float32)
    r = np.arange(72)
    trows[r // 9 * 16 + r % 9, r] = 1
    col = tb[None, :] == np.arange(12)[:, None]
    lev = (ta[None, None, :] == np.arange(6)[:, None, None]) & (tl[None, None, :] == np.arange(2)[None, :, None])
    return [
        np.ascontiguousarray(m).astype(ml_dtypes.bfloat16)
        for m in (rep, heads, shift, trows, col, lev)
    ]


def mm(a, b):
    return lax.dot_general(a, b, (((1,), (0,)), ((), ())), preferred_element_type=F32)


def mmt(a, b):
    return lax.dot_general(a, b, (((1,), (1,)), ((), ())), preferred_element_type=F32)


def mtm(a, b):
    return lax.dot_general(a, b, (((0,), (0,)), ((), ())), preferred_element_type=F32)


def kernel(
    x_hbm, g_hbm, gain_hbm, wqkv_hbm, wproj_hbm, table_hbm, regions_hbm,
    rep_hbm, heads_hbm, shift_hbm, trows_hbm, col_hbm, lev_hbm,
    out_x, out_qkv, out_proj, out_gain, out_table,
    gain_ref, wqkv_ref, wproj_ref, table_ref, regions_ref,
    rep_ref, heads_ref, shift_ref, trows_ref, col_ref, lev_ref,
    own_x, own_g, reg_s, reg_r, pack, win, gxw, orecv, xg, gx, t1, t2, bm,
    main_f, main_s, main_r, xy_f, xy_s, xy_r, za, zb, fin,
    tcx_s, tcx_r, ta, tb, tfin, sq,
    load_sem, reg_ss, reg_rs, halo_ss, halo_rs, ret_ss, ret_rs, core_ss, core_rs, xy_ss, xy_rs, za_ss, za_rs, zb_ss, zb_rs,
    xyag_ss, xyag_rs, cag_ss, cag_rs,
    tcx_ss, tcx_rs, ta_ss, ta_rs, tb_ss, tb_rs, tcag_ss, tcag_rs, sq_ss, sq_rs, far_sem, band_sem,
):
    lat = lax.axis_index("lat")
    lon = lax.axis_index("lon")
    nlat, nlon = NLAT, NX * ZLO * 2
    y, z_hi = lat // ZHI, lax.rem(lat, ZHI)
    core = lax.rem(lon, 2)
    chip = lon // 2
    x, z_lo = chip // ZLO, lax.rem(chip, ZLO)
    zq, zr = z_hi * 2 + z_lo // 4, lax.rem(z_lo, 4)
    zhalf = z_lo // 4
    p = x * NY + y
    cx = x * 2 + core

    def lon_of(x_, z_lo_, core_):
        return (x_ * ZLO + z_lo_) * 2 + core_

    core_peer = (lat, lon_of(x, z_lo, 1 - core))

    def xy_peer(o):
        other = lax.rem(p + o, NXY)
        return other, ((other // NY) * 0 + lax.rem(other, NY) * ZHI + z_hi, lon_of(other // NY, z_lo, core))

    def zr_peer(o):
        return (lat, lon_of(x, zhalf * 4 + lax.rem(zr + o, 4), core))

    def zq_peer(o):
        other = lax.rem(zq + o, 4)
        return (y * ZHI + other // 2, lon_of(x, lax.rem(other, 2) * 4 + zr, core))

    def cx_peer(o):
        other = lax.rem(cx + o, NCX)
        return other, (lat, lon_of(other // 2, z_lo, lax.rem(other, 2)))

    far_half = (lat, lon_of(x, lax.rem(z_lo + 4, ZLO), core))
    owner = jnp.logical_or(x != y, x == 0)
    w = jnp.where(x == y, PIECES - 1, x * (NY - 1) + y - (y > x).astype(jnp.int32))

    def place(n):
        i, j = OWNERS[n]
        return i * NY + j, (j * ZHI + z_hi, lon_of(i, z_lo, core))

    def lat_peer(o):
        return (lax.rem(lat + o, NLAT), lon)

    def midway(lat_, lon_):
        chip_ = lon_ // 2
        x_, z_ = chip_ // ZLO, lax.rem(chip_, ZLO)
        return (lat_, lon_of(x_, lax.rem(z_ + 4, ZLO), lax.rem(lon_, 2)))

    def to_window(ah, bh):
        return midway(lax.rem(lat + nlat - ah, nlat), lax.rem(lon + nlon - bh, nlon))

    def from_window(ah, bh):
        return (lax.rem(lat + ah, nlat), lax.rem(midway(lat, lon)[1] + bh, nlon))

    barrier = pltpu.get_barrier_semaphore()

    def greet(device):
        pl.semaphore_signal(barrier, inc=1, device_id=device, device_id_type=MESH)

    pairs = (
        (x_hbm, own_x), (g_hbm, own_g), (regions_hbm, regions_ref), (col_hbm, col_ref), (lev_hbm, lev_ref),
        (table_hbm, table_ref), (shift_hbm, shift_ref), (rep_hbm, rep_ref), (heads_hbm, heads_ref),
        (wqkv_hbm, wqkv_ref), (wproj_hbm, wproj_ref), (gain_hbm, gain_ref),
        (trows_hbm, trows_ref),
    )
    loads = [pltpu.make_async_copy(src, dst, load_sem.at[n]) for n, (src, dst) in enumerate(pairs)]
    for c in loads[:2]:
        c.start()

    quarters = ((1, 1), (1, 0), (0, 1), (0, 0))
    for ah, bh in quarters:
        greet(from_window(ah, bh))
    for ah, bh in quarters:
        greet(to_window(ah, bh))
    greet(zq_peer(1))
    greet(zq_peer(3))
    steps = [(i, j) for i in range(NX) for j in range(NY) if (i, j) != (0, 0)]
    for i, j in sorted(steps, key=lambda d: -(min(d[0], NX - d[0]) + min(d[1], NY - d[1]))):
        greet((lax.rem(y + j, NY) * ZHI + z_hi, lon_of(lax.rem(x + i, NX), z_lo, core)))
    for o in range(1, 4):
        greet((lat, lon_of(lax.rem(x + o, NX), z_lo, 1 - core)))
    for o in range(1, 4):
        greet(zr_peer(o))
    greet(core_peer)
    for c in loads[2:]:
        c.start()

    for c in loads[:5]:
        c.wait()
    reg_row = jnp.zeros((1, 144), F32)
    for i in range(6):
        reg = regions_ref[i].astype(F32).astype(BF)
        reg_row += jnp.sum(mm(reg, col_ref[...]) * lev_ref[i].astype(F32), axis=0, keepdims=True)
    reg_s[...] = reg_row

    pack[:, :, 0] = own_x[:, :, :, 0:128]
    pack[:, :, 1] = own_g[:, :, :, 0:128]
    pack[:, :, 2] = jnp.concatenate([own_x[:, :, :, 128:192], own_g[:, :, :, 128:192]], axis=-1)

    pl.semaphore_wait(barrier, 8 + 2 + (NXY - 1) + 3 + 3 + 1)

    def remote(src, dst, ss, rs, device):
        return pltpu.make_async_remote_copy(
            src_ref=src, dst_ref=dst, send_sem=ss, recv_sem=rs, device_id=device, device_id_type=MESH
        )

    def here(ah, bh):
        return pl.ds(3 - 3 * ah, 3), pl.ds(6 - 6 * bh, 6)

    def there(ah, bh):
        return pl.ds(3 * ah, 3), pl.ds(6 * bh, 6)

    halo = [remote(reg_s, reg_r, reg_ss, reg_rs, midway(lat, lon))]
    for ah, bh in quarters:
        at = ah * 2 + bh
        halo.append(remote(
            pack.at[here(ah, bh)], win.at[there(ah, bh)], halo_ss.at[at], halo_rs.at[at], to_window(ah, bh)
        ))
    for c in halo:
        c.start()
    pl.semaphore_signal(far_sem, inc=1, device_id=zq_peer(3), device_id_type=MESH)

    for c in loads[5:]:
        c.wait()
    t2[...] = jnp.zeros_like(t2)
    for h in range(6):
        t1[h:h + 1, :] = table_ref[h]
    for l_s in range(2):
        for a_s in range(6):
            la = l_s * 6 + a_s
            for l_t in range(2):
                off = l_s * 1656 + l_t * 828 + a_s * 138
                t2[pl.ds(la * 6, 6), pl.ds(l_t * 138, 138)] = t1[:, pl.ds(off, 138)]
    t_all = t2[...]
    t_hi = t_all.astype(BF)
    t_rest = t_all - t_hi.astype(F32)
    t_mid = t_rest.astype(BF)
    t_lo = (t_rest - t_mid.astype(F32)).astype(BF)

    for b in range(12):
        sel = shift_ref[b]
        bm[pl.ds(b * 72, 72), :] = mmt(t_hi, sel) + mmt(t_mid, sel) + mmt(t_lo, sel)
    rep = rep_ref[...]
    heads = heads_ref[...]
    heads_f = heads.astype(F32)

    halo[0].wait_recv()
    kind = lax.broadcasted_iota(jnp.int32, (8, 144), 0).astype(F32)
    which = (reg_r[...] == kind).astype(F32).astype(BF)
    keep = mm(mmt(rep, which).astype(BF), which)

    for c in halo[1:]:
        c.wait_recv()
    for n in range(72):
        for c in range(3):
            xg[2 * n:2 * n + 2, c * 128:c * 128 + 128] = win[n // 12, n % 12, c]
    high = xg[:, 256:384].astype(F32)
    win_x = jnp.concatenate([xg[:, 0:128].astype(F32), high[:, 0:64]], axis=1)
    win_g = jnp.concatenate([xg[:, 128:256].astype(F32), high[:, 64:128]], axis=1).astype(BF)

    gain = gain_ref[...]
    mean = jnp.mean(win_x, axis=-1, keepdims=True)
    centred = win_x - mean
    inv_std = lax.rsqrt(jnp.mean(centred * centred, axis=-1, keepdims=True) + EPS_NORM)
    standard = centred * inv_std
    normed = (standard * gain).astype(BF)
    projected = mm(normed, wqkv_ref[...])
    q = projected[:, 0:192].astype(BF)
    k = projected[:, 192:384].astype(BF)
    v = projected[:, 384:576].astype(BF)
    grad_mixed = mmt(win_g, wproj_ref[...]).astype(BF)

    qm = (mm(rep, q) * heads_f).astype(BF)
    gm = (mm(rep, grad_mixed) * heads_f).astype(BF)
    scores = jnp.where(keep > 0.5, mmt(qm, k) * SCALE + bm[...], -1e30)
    top = jnp.max(scores, axis=-1, keepdims=True)
    e = jnp.exp(scores - top)
    probs = e / jnp.sum(e, axis=-1, keepdims=True)
    probs_low = probs.astype(BF)
    grad_probs = mmt(gm, v)
    grad_scores = probs * (grad_probs - jnp.sum(probs * grad_probs, axis=-1, keepdims=True))
    gs_low = grad_scores.astype(BF)
    mixed = mtm(rep, (mm(probs_low, v) * heads_f).astype(BF)).astype(BF)
    gq = mtm(rep, (mm(gs_low, k) * SCALE * heads_f).astype(BF))
    gk = mtm(gs_low, qm) * SCALE
    gv = mtm(probs_low, gm)
    gpi = jnp.concatenate([gq, gk, gv], axis=1).astype(BF)

    g_qkv = mtm(normed, gpi)
    main_f[0] = g_qkv[:, 0:384]
    main_f[1] = jnp.concatenate([g_qkv[:, 384:576], mtm(mixed, win_g)], axis=1)
    main_s[...] = main_f[1 - core].astype(BF)
    core_rs_copy = remote(main_s, main_r, core_ss, core_rs, core_peer)
    core_rs_copy.start()

    grad_normed = mmt(gpi, wqkv_ref[...])
    gain_raw = jnp.sum(grad_normed * standard, axis=0, keepdims=True)
    core_rs_copy.wait_recv()
    both_cores = main_f[core] + main_r[...].astype(F32)
    xy_f[0:PIECES - 1] = both_cores.reshape(PIECES - 1, 16, 384)
    xy_f[PIECES - 1] = jnp.zeros((16, 384), F32)
    xy_f[PIECES - 1, 0:1, 0:192] = gain_raw
    xy_s[...] = xy_f[...].astype(BF)
    xy_r[p] = jnp.zeros((16, 384), BF)

    def xy_copy(n):
        at, device = place(n)
        return at, remote(xy_s.at[n], xy_r.at[p], xy_ss.at[n], xy_rs.at[p], device)

    for n in range(PIECES):
        at, c = xy_copy(n)

        @pl.when(p != at)
        def _(c=c):
            c.start()

    t_acc = jnp.zeros((72, 384), F32)
    for b in range(12):
        t_acc += mm(gs_low[b * 72:(b + 1) * 72, :], shift_ref[b])
    tcx_s[...] = mm(trows_ref[...], t_acc.astype(BF)).astype(BF).reshape(8, 16, 384)

    def tcx_copy(o):
        other, device = cx_peer(o)
        return remote(tcx_s.at[other], tcx_r.at[o - 1], tcx_ss.at[o - 1], tcx_rs.at[o - 1], device)

    @pl.loop(1, NCX)
    def _(o):
        tcx_copy(o).start()

    grad_std = grad_normed * gain
    grad_x = inv_std * (
        grad_std
        - jnp.mean(grad_std, axis=-1, keepdims=True)
        - standard * jnp.mean(grad_std * standard, axis=-1, keepdims=True)
    )
    gx[...] = grad_x.astype(BF)
    for n in range(72):
        gxw[n // 12, n % 12] = gx[2 * n:2 * n + 2, :]
    ret_copies = [
        remote(gxw.at[there(ah, bh)], orecv.at[here(ah, bh)], ret_ss.at[ah * 2 + bh], ret_rs.at[ah * 2 + bh], from_window(ah, bh))
        for ah, bh in quarters
    ]

    for c in halo + [core_rs_copy]:
        c.wait_send()

    @pl.loop(1, NCX)
    def _(o):
        tcx_copy(o).wait_recv()

    tacc = tcx_s[cx].astype(F32)
    for o in range(NCX - 1):
        tacc += tcx_r[o].astype(F32)
    ta[zr] = tacc.astype(BF)

    def spread(buf, at, ss, rs, peer, n):
        out = [remote(buf.at[at], buf.at[at], ss.at[o - 1], rs.at[o - 1], peer(o)) for o in range(1, n)]
        into = []
        for o in range(1, n):
            slot = buf.at[lax.rem(at + n - o, n)]
            into.append(remote(slot, slot, ss.at[o - 1], rs.at[o - 1], peer(o)))
        return out, into

    ta_out, ta_in = spread(ta, zr, ta_ss, ta_rs, zr_peer, 4)
    for c in ta_out:
        c.start()

    za_out, za_in = spread(za, zr, za_ss, za_rs, zr_peer, 4)

    @pl.when(owner)
    def _():
        for j in range(NXY):
            @pl.when(p != j)
            def _(j=j):
                remote(xy_s.at[0], xy_r.at[j], xy_ss.at[0], xy_rs.at[j], core_peer).wait_recv()

        acc = xy_f[w]
        for j in range(NXY):
            acc += xy_r[j].astype(F32)
        za[zr] = acc.astype(BF)
        for c in za_out:
            c.start()

    for c in ta_in:
        c.wait_recv()
    tsum = ta[0].astype(F32)
    for j in range(1, 4):
        tsum += ta[j].astype(F32)
    tb[zhalf] = tsum.astype(BF)
    tb_out, tb_in = spread(tb, zhalf, tb_ss, tb_rs, lambda o: far_half, 2)
    tb_out[0].start()

    pl.semaphore_wait(far_sem, 1)
    for o in range(1, NY):
        pl.semaphore_signal(
            band_sem, inc=1, device_id=(lax.rem(y + o, NY) * ZHI + z_hi, lon), device_id_type=MESH
        )

    zb_out, zb_in = spread(zb, zq, zb_ss, zb_rs, zq_peer, 4)

    @pl.when(owner)
    def _():
        for c in za_in:
            c.wait_recv()
        acc = za[0].astype(F32)
        for j in range(1, 4):
            acc += za[j].astype(F32)
        zb[zq] = acc.astype(BF)
        for c in (zb_out[1], zb_out[0], zb_out[2]):
            c.start()

    for c in ret_copies:
        c.start()

    tb_in[0].wait_recv()
    tfin[cx] = (tb[0].astype(F32) + tb[1].astype(F32)).astype(BF)

    def tcag_copy(o):
        _, device = cx_peer(o)
        return remote(tfin.at[cx], tfin.at[cx], tcag_ss.at[o - 1], tcag_rs.at[o - 1], device)

    @pl.loop(1, NCX)
    def _(o):
        tcag_copy(o).start()

    for n in range(PIECES):
        at, c = xy_copy(n)

        @pl.when(p != at)
        def _(c=c):
            c.wait_send()

    @pl.loop(1, NCX)
    def _(o):
        tcx_copy(o).wait_send()

    for c in ta_out + tb_out:
        c.wait_send()

    @pl.loop(1, NCX)
    def _(o):
        other = lax.rem(cx + NCX - o, NCX)
        slot = tfin.at[other]
        remote(slot, slot, tcag_ss.at[o - 1], tcag_rs.at[o - 1], cx_peer(o)[1]).wait_recv()

    def squares_of(value):
        return jnp.sum(jnp.sum(value * value, axis=1, keepdims=True), axis=0, keepdims=True)

    band = mtm(trows_ref[...], tfin[...].reshape(128, 384))
    sq[lat] = jnp.broadcast_to(squares_of(band), (1, 128))
    sq_out, sq_in = spread(sq, lat, sq_ss, sq_rs, lat_peer, NLAT)
    pl.semaphore_wait(band_sem, NY - 1)
    for c in sq_out:
        c.start()

    def xyag_copy(o):
        _, device = xy_peer(o)
        return remote(fin.at[core, w], fin.at[core, w], xyag_ss.at[o - 1], xyag_rs.at[w], device)

    @pl.when(owner)
    def _():
        for c in za_out:
            c.wait_send()
        for c in zb_in:
            c.wait_recv()
        acc = zb[0].astype(F32)
        for j in range(1, 4):
            acc += zb[j].astype(F32)
        fin[core, w] = acc.astype(BF)

        @pl.loop(1, NXY)
        def _(o):
            xyag_copy(o).start()

    for c in ret_copies:
        c.wait()
    out_x[...] = (own_g[...].astype(F32) + orecv[...].astype(F32)).astype(BF)

    @pl.loop(1, NCX)
    def _(o):
        tcag_copy(o).wait_send()

    @pl.when(owner)
    def _():
        for c in zb_out:
            c.wait_send()

    for n in range(PIECES):
        at, device = place(n)

        @pl.when(p != at)
        def _(n=n, device=device):
            slot = fin.at[core, n]
            remote(slot, slot, xyag_ss.at[0], xyag_rs.at[n], device).wait_recv()

    cag = remote(fin.at[core], fin.at[core], cag_ss, cag_rs, core_peer)
    cag.start()

    @pl.when(owner)
    def _():
        @pl.loop(1, NXY)
        def _(o):
            xyag_copy(o).wait_send()

    for c in sq_in:
        c.wait_recv()
    total = sq[0]
    for j in range(1, NLAT):
        total += sq[j]
    total = total[:, 0:1]
    band = band * (1.0 / jnp.sqrt(total / (NLAT * 6 * 3312) + EPS_RMS))
    for l_s in range(2):
        for a_s in range(6):
            la = l_s * 6 + a_s
            for l_t in range(2):
                off = l_s * 1656 + l_t * 828 + a_s * 138
                t1[:, pl.ds(off, 138)] = band[la * 6:la * 6 + 6, l_t * 138:l_t * 138 + 138]
    for h in range(6):
        out_table[h] = t1[h:h + 1, :]
    for c in sq_out:
        c.wait_send()

    def part(which_core):
        value = fin[which_core, 0:PIECES - 1].reshape(192, 384).astype(F32)
        return value, squares_of(value[:, 0:192]), squares_of(value[:, 192:384]), fin[which_core, PIECES - 1, 0:1, 0:192].astype(F32)

    own = part(core)
    other_half = fin.at[1 - core]
    remote(other_half, other_half, cag_ss, cag_rs, core_peer).wait_recv()
    theirs = part(1 - core)
    first = [jnp.where(core == 0, a, b) for a, b in zip(own, theirs)]
    second = [jnp.where(core == 0, b, a) for a, b in zip(own, theirs)]

    def scale_of(total, entries):
        return 1.0 / jnp.sqrt(total / entries + EPS_RMS)

    s_qkv = scale_of(first[1] + first[2] + second[1], 192 * 576)
    s_proj = scale_of(second[2], 192 * 192)
    out_qkv[:, 0:384] = first[0] * s_qkv
    out_qkv[:, 384:576] = second[0][:, 0:192] * s_qkv
    out_proj[...] = second[0][:, 192:384] * s_proj
    w_g = first[3] + second[3]
    out_gain[...] = w_g * scale_of(squares_of(w_g), 192)
    cag.wait_send()


def hand_over(*refs):
    sem = refs[-1]
    n = (len(refs) - 1) // 2
    copies = [pltpu.make_async_copy(refs[i], refs[n + i], sem.at[i]) for i in range(n)]
    for c in copies:
        c.start()
    for c in copies:
        c.wait()


def on_device(activations, cotangent, gain, w_qkv, w_proj, bias_table, regions):
    consts = [jnp.asarray(m) for m in tables()]
    vmem = pl.BlockSpec(memory_space=pltpu.VMEM)
    hbm = pl.BlockSpec(memory_space=pltpu.HBM)
    dma = pltpu.SemaphoreType.DMA
    operands = [
        activations.transpose(1, 2, 0, 3), cotangent.transpose(1, 2, 0, 3), gain.reshape(1, 192), w_qkv, w_proj,
        bias_table.transpose(1, 0, 2), regions.transpose(1, 0, 2), *consts,
    ]
    scratch = [pltpu.VMEM(o.shape, o.dtype) for o in operands[2:]] + [
        pltpu.VMEM((6, 12, 2, 192), BF), pltpu.VMEM((6, 12, 2, 192), BF), pltpu.VMEM((1, 144), F32), pltpu.VMEM((1, 144), F32),
        pltpu.VMEM((6, 12, 3, 2, 128), BF), pltpu.VMEM((6, 12, 3, 2, 128), BF),
        pltpu.VMEM((6, 12, 2, 192), BF), pltpu.VMEM((6, 12, 2, 192), BF),
        pltpu.VMEM((144, 384), BF), pltpu.VMEM((144, 192), BF),
        pltpu.VMEM((6, 3312), F32), pltpu.VMEM((72, 384), F32), pltpu.VMEM((864, 144), F32),
        pltpu.VMEM((2, 192, 384), F32), pltpu.VMEM((192, 384), BF), pltpu.VMEM((192, 384), BF),
        pltpu.VMEM((PIECES, 16, 384), F32), pltpu.VMEM((PIECES, 16, 384), BF), pltpu.VMEM((16, 16, 384), BF),
        pltpu.VMEM((4, 16, 384), BF), pltpu.VMEM((4, 16, 384), BF), pltpu.VMEM((2, PIECES, 16, 384), BF),
        pltpu.VMEM((8, 16, 384), BF), pltpu.VMEM((7, 16, 384), BF),
        pltpu.VMEM((4, 16, 384), BF), pltpu.VMEM((2, 16, 384), BF),
        pltpu.VMEM((8, 16, 384), BF), pltpu.VMEM((NLAT, 1, 128), F32),
        dma((13,)), dma, dma, dma((4,)), dma((4,)), dma((4,)), dma((4,)), dma, dma,
        dma((PIECES,)), dma((16,)), dma((3,)), dma((3,)), dma((3,)), dma((3,)),
        dma((15,)), dma((PIECES,)), dma, dma,
        dma((7,)), dma((7,)), dma((3,)), dma((3,)), dma((1,)), dma((1,)), dma((7,)), dma((7,)), dma((7,)), dma((7,)),
        pltpu.SemaphoreType.REGULAR, pltpu.SemaphoreType.REGULAR,
    ]
    shapes = (
        jax.ShapeDtypeStruct((6, 12, 2, 192), BF),
        jax.ShapeDtypeStruct((192, 576), F32),
        jax.ShapeDtypeStruct((192, 192), F32),
        jax.ShapeDtypeStruct((1, 192), F32),
        jax.ShapeDtypeStruct((6, 1, 3312), F32),
    )
    outs = pl.pallas_call(
        kernel,
        out_shape=shapes,
        in_specs=[hbm] * len(operands),
        out_specs=(vmem,) * 5,
        scratch_shapes=scratch,
        compiler_params=pltpu.CompilerParams(
            collective_id=0, has_side_effects=True, vmem_limit_bytes=40 * 1024 * 1024
        ),
        name="swin_backward",
    )(*[pltpu.with_memory_space_constraint(o, pltpu.HBM) for o in operands])
    outs = pl.pallas_call(
        hand_over,
        out_shape=shapes,
        in_specs=[vmem] * 5,
        out_specs=(hbm,) * 5,
        scratch_shapes=[dma((5,))],
        compiler_params=pltpu.CompilerParams(vmem_limit_bytes=32 * 1024 * 1024),
        name="hand_over",
    )(*outs)
    return outs[0].transpose(2, 0, 1, 3), outs[1], outs[2], outs[3].reshape(192), outs[4].transpose(1, 0, 2)


def solution(mesh):
    in_specs = (
        P(None, "lat", "lon", None),
        P(None, "lat", "lon", None),
        P(),
        P(),
        P(),
        P("lat", None, None),
        P(None, "lat", "lon"),
    )
    out_specs = (P(None, "lat", "lon", None), P(), P(), P(), P("lat", None, None))
    return jax.shard_map(
        on_device, mesh=mesh, in_specs=in_specs, out_specs=out_specs, check_vma=False
    )
```
